32 devices in a mesh: grp: 4 (over x, core), box: 8 (over z, y).
Axes of the slice: x: 2, y: 2, z: 4, core: 2. Of those that a mesh axis runs over, the one named last changes fastest.
Arguments:
- right_side: float32 [64, 256, 128], P('grp', 'box'), may hold values from -6 to 6
- beta: float32 [64, 256, 128], P('grp', 'box'), may hold values from 0.25 to 4
Outputs:
- correction: float32 [64, 256, 128], P('grp', 'box')
The draws below stay inside these ranges and needn't reach their ends.
All inputs are finite; a program needn't handle non-finite values.
Results may differ from the reference program's by a relative error of at most 0.0001.
Values sent between devices are 32-bit elements; how exact they have to be, the bound alone decides.
A program may use at most 64 MiB of HBM per device.

```python
import math
import jax
import jax.numpy as jnp

LEVELS = 4
SWEEPS = 2
COARSE = 8
NX = 64
NY = 256
NZ = 128


def draw_right_side(key, part):
    return jnp.clip(jax.random.normal(key, (NX, NY, NZ), jnp.float32), -6.0, 6.0)


def block_scale(key, dims, cuts, least, high):
    def one(axis_at, parts):
        draws = jax.random.uniform(jax.random.fold_in(jax.random.fold_in(key, 6), axis_at), (parts,), jnp.float32, least / len(cuts), high / len(cuts))
        return jnp.repeat(jnp.exp(draws), dims[axis_at] // parts).reshape((-1,) + (1,) * (len(dims) - axis_at - 1))

    level = one(*cuts[0])
    for cut in cuts[1:]:
        level = level * one(*cut)
    return level


def setup_inputs(seed: int = 0) -> dict:
    splits = jax.random.split(jax.random.key(seed), 3)
    right_side = draw_right_side(jax.random.fold_in(splits[2], 71), 0)
    beta = jnp.clip(jnp.exp(math.log(4.0) - 2.7725887 * jax.random.uniform(splits[1], (NX, NY, NZ), jnp.float32) ** block_scale(splits[1], (NX, NY, NZ), ((0, 4), (1, 8)), -0.2, 0.2)), 0.25, 4.0)
    return dict(right_side=right_side, beta=beta)


relax_weight = 2.0 / 3.0


def pad_zeros(field):
    return jnp.pad(field, 1)


def face_coeffs(padded_beta):
    face_x = 0.5 * (padded_beta[1:, 1:-1, 1:-1] + padded_beta[:-1, 1:-1, 1:-1])
    face_y = 0.5 * (padded_beta[1:-1, 1:, 1:-1] + padded_beta[1:-1, :-1, 1:-1])
    face_z = 0.5 * (padded_beta[1:-1, 1:-1, 1:] + padded_beta[1:-1, 1:-1, :-1])
    return face_x, face_y, face_z


def inverse_diagonal(coeffs, scale):
    face_x, face_y, face_z = coeffs
    total = face_x[:-1] + face_x[1:] + face_y[:, :-1] + face_y[:, 1:] + face_z[:, :, :-1] + face_z[:, :, 1:]
    return 1.0 / (scale * total)


def apply_operator(padded, coeffs, scale):
    face_x, face_y, face_z = coeffs
    centre = padded[1:-1, 1:-1, 1:-1]
    total = face_x[:-1] * (centre - padded[:-2, 1:-1, 1:-1]) + face_x[1:] * (centre - padded[2:, 1:-1, 1:-1])
    total = total + face_y[:, :-1] * (centre - padded[1:-1, :-2, 1:-1]) + face_y[:, 1:] * (centre - padded[1:-1, 2:, 1:-1])
    total = total + face_z[:, :, :-1] * (centre - padded[1:-1, 1:-1, :-2]) + face_z[:, :, 1:] * (centre - padded[1:-1, 1:-1, 2:])
    return scale * total


def jacobi_sweeps(field, source, coeffs, inverse, scale, count):
    for sweep_index in range(count):
        field = field + relax_weight * (source - apply_operator(pad_zeros(field), coeffs, scale)) * inverse
    return field


def conjugate_solve(source, coeffs, scale, count):
    field = jnp.zeros_like(source)
    remain = source
    direction = source
    norm_now = jnp.sum(remain * remain)
    for step_index in range(count):
        image = apply_operator(pad_zeros(direction), coeffs, scale)
        alpha = norm_now / jnp.sum(direction * image)
        field = field + alpha * direction
        remain = remain - alpha * image
        norm_next = jnp.sum(remain * remain)
        direction = remain + (norm_next / norm_now) * direction
        norm_now = norm_next
    return field


def restrict_mean(field):
    size_a, size_b, size_c = field.shape
    blocks = field.reshape(size_a // 2, 2, size_b // 2, 2, size_c // 2, 2)
    return jnp.mean(blocks, axis=(1, 3, 5))


def prolong_copy(field):
    return jnp.repeat(jnp.repeat(jnp.repeat(field, 2, axis=0), 2, axis=1), 2, axis=2)


def reference(right_side, beta):
    sources = [right_side]
    betas = [beta]
    saved = []
    for level in range(LEVELS):
        scale = 0.25 ** level
        coeffs = face_coeffs(pad_zeros(betas[level]))
        inverse = inverse_diagonal(coeffs, scale)
        field = jacobi_sweeps(jnp.zeros_like(sources[level]), sources[level], coeffs, inverse, scale, SWEEPS)
        residual = sources[level] - apply_operator(pad_zeros(field), coeffs, scale)
        saved.append((field, coeffs, inverse, scale))
        sources.append(restrict_mean(residual))
        betas.append(restrict_mean(betas[level]))
    low_scale = 0.25 ** LEVELS
    low_coeffs = face_coeffs(pad_zeros(betas[LEVELS]))
    field = conjugate_solve(sources[LEVELS], low_coeffs, low_scale, COARSE)
    for level in range(LEVELS - 1, -1, -1):
        kept, coeffs, inverse, scale = saved[level]
        field = kept + prolong_copy(field)
        field = jacobi_sweeps(field, sources[level], coeffs, inverse, scale, SWEEPS)
    return field
```

```python
import functools

import jax
import jax.numpy as jnp
from jax import lax
from jax.experimental import pallas as pl
from jax.experimental.pallas import tpu as pltpu
from jax.sharding import PartitionSpec as P

LEVELS = 4
SWEEPS = 2
COARSE = 8
W = 2.0 / 3.0
MESH = pl.DeviceIdType.MESH
F32 = jnp.float32

X0, Y0, LANES = 16, 32, 128
H0 = 4
H1 = 5
HY = 8
DIRS = [(dx, dy) for dx in (-1, 0, 1) for dy in (-1, 0, 1) if (dx, dy) != (0, 0)]


def roll(v, shift, axis):
    return pltpu.roll(v, shift % v.shape[axis], axis)


def lane_of(shape):
    return lax.broadcasted_iota(jnp.int32, shape, len(shape) - 1)


def pair_lanes(v, apart):
    lane = lane_of(v.shape)
    return v + jnp.where((lane & apart) == 0, roll(v, -apart, 1), roll(v, apart, 1))


def span(size, halo, step, own):
    if step == 0:
        return (halo, size), (halo, size)
    if step < 0:
        return (halo, own), (halo + size, own)
    return (halo + size - own, own), (0, own)


def kernel(
    G, B, rs_ref, be_ref, out_ref,
    B0, S0, V0, U0, CX0, CY0, CM0, CP0, Q0, D0,
    B1, S1, V1, U1, CX1, CY1, CM1, CP1, Q1, D1,
    T, PB, PS, GB, GS, V2, C2, C3, C4, E, F3,
    halo_send, halo_recv, ga_send, ga_recv, own_sem, loc_sem,
):
    n = G * B
    g = lax.axis_index("grp")
    b = lax.axis_index("box")
    me = g * B + b
    ry2, ry3, ry4 = 8 * B, 4 * B, 2 * B

    own0 = (pl.ds(H0, X0), pl.ds(HY, Y0))
    load_b = pltpu.make_async_copy(be_ref, B0.at[own0[0], own0[1]], loc_sem.at[0])
    load_s = pltpu.make_async_copy(rs_ref, S0.at[own0[0], own0[1]], loc_sem.at[1])
    load_b.start()
    load_s.start()

    barrier = pltpu.get_barrier_semaphore()

    def greet(d, carry):
        peer = (me + d) % n
        pl.semaphore_signal(barrier, inc=1, device_id=(peer // B, peer % B), device_id_type=MESH)
        return carry

    lax.fori_loop(1, n, greet, 0)

    for ref, nx, hx, ny in ((B0, X0, H0, Y0), (S0, X0, H0, Y0), (B1, X0 // 2, H1, Y0 // 2), (S1, X0 // 2, H1, Y0 // 2)):
        rows = ny + 2 * HY
        planes = nx + 2 * hx

        @pl.when(g == 0)
        def _():
            ref[pl.ds(0, hx)] = jnp.zeros((hx, rows, LANES), F32)

        @pl.when(g == G - 1)
        def _():
            ref[pl.ds(hx + nx, hx)] = jnp.zeros((hx, rows, LANES), F32)

        @pl.when(b == 0)
        def _():
            ref[:, pl.ds(0, HY)] = jnp.zeros((planes, HY, LANES), F32)

        @pl.when(b == B - 1)
        def _():
            ref[:, pl.ds(HY + ny, HY)] = jnp.zeros((planes, HY, LANES), F32)

    V2[0] = jnp.zeros((ry2 + 16, LANES), F32)
    V2[G + 1] = jnp.zeros((ry2 + 16, LANES), F32)
    V2[:, pl.ds(0, 8)] = jnp.zeros((G + 2, 8, LANES), F32)
    V2[:, pl.ds(8 + ry2, 8)] = jnp.zeros((G + 2, 8, LANES), F32)

    pl.semaphore_wait(barrier, n - 1)

    def halo_copies(kind, src, dst, nx, hx, ny, src_is_input):
        made = []
        for at, (dx, dy) in enumerate(DIRS):
            (sx, lx), (tx, _) = span(nx, hx, dx, hx)
            (sy, ly), (ty, _) = span(ny, HY, dy, HY)
            if src_is_input:
                sx, sy = sx - hx, sy - HY
            copy = pltpu.make_async_remote_copy(
                src_ref=src.at[pl.ds(sx, lx), pl.ds(sy, ly)],
                dst_ref=dst.at[pl.ds(tx, lx), pl.ds(ty, ly)],
                send_sem=halo_send.at[kind, at],
                recv_sem=halo_recv.at[kind, at],
                device_id=(g + dx, b + dy),
                device_id_type=MESH,
            )
            there = (g + dx >= 0) & (g + dx < G) & (b + dy >= 0) & (b + dy < B)
            here = (g - dx >= 0) & (g - dx < G) & (b - dy >= 0) & (b - dy < B)
            made.append((copy, there, here))
        return made

    def start_all(copies):
        for copy, there, _ in copies:
            pl.when(there)(copy.start)

    def recv_all(copies):
        for copy, _, here in copies:
            pl.when(here)(copy.wait_recv)

    def sent_all(copies):
        for copy, there, _ in copies:
            pl.when(there)(copy.wait_send)

    def gather_start(which, packed, whole):
        pltpu.make_async_copy(packed, whole.at[g, pl.ds(pl.multiple_of(b * 8, 8), 8)], ga_recv.at[which]).start()

        def one(d, carry):
            peer = (me + d) % n
            pltpu.make_async_remote_copy(
                src_ref=packed,
                dst_ref=whole.at[g, pl.ds(pl.multiple_of(b * 8, 8), 8)],
                send_sem=ga_send.at[which, d],
                recv_sem=ga_recv.at[which],
                device_id=(peer // B, peer % B),
                device_id_type=MESH,
            ).start()
            return carry

        lax.fori_loop(1, n, one, 0)

    def gather_recv(which, whole):
        pltpu.make_async_copy(whole, whole, ga_recv.at[which]).wait()

    def gather_sent(which, packed):
        def one(d, carry):
            pltpu.make_async_copy(packed, packed, ga_send.at[which, d]).wait()
            return carry

        lax.fori_loop(1, n, one, 0)

    beta_halo = halo_copies(0, be_ref, B0, X0, H0, Y0, True)
    source_halo = halo_copies(1, rs_ref, S0, X0, H0, Y0, True)
    start_all(beta_halo)
    start_all(source_halo)
    load_b.wait()

    def halve(pair, apart, slot):
        rows = pair.shape[0]
        T[slot, pl.ds(0, rows)] = pair_lanes(pair, apart)
        return 0.125 * (T[slot, pl.ds(0, rows // 2, stride=2)] + T[slot, pl.ds(1, rows // 2, stride=2)])

    def pack(planes):
        lane = lane_of(planes[0].shape) & 3
        packed = planes[3]
        for k in (2, 1, 0):
            packed = jnp.where(lane == k, planes[k], packed)
        return packed

    for p in range(X0 // 2):
        B1[H1 + p, pl.ds(HY, Y0 // 2)] = halve(
            B0[H0 + 2 * p, pl.ds(HY, Y0)] + B0[H0 + 2 * p + 1, pl.ds(HY, Y0)], 1, p
        )
    beta1_halo = halo_copies(2, B1, B1, X0 // 2, H1, Y0 // 2, False)
    start_all(beta1_halo)
    PB[...] = pack([
        halve(B1[H1 + 2 * p, pl.ds(HY, Y0 // 2)] + B1[H1 + 2 * p + 1, pl.ds(HY, Y0 // 2)], 2, p)
        for p in range(X0 // 4)
    ])
    gather_start(0, PB, GB)

    def setup(level, Bl, CX, CY, CM, CP, Q, D, first, last, row, rows, hx, nx, ny):
        apart = 1 << level
        h = 0.5 * 0.25**level

        def plane(i, carry):
            at = pl.ds(row, rows)
            c = Bl[i, at]
            xm = Bl[i - 1, at]
            xp = Bl[i + 1, at]
            ym = Bl[i, pl.ds(row - 1, rows)]
            yp = Bl[i, pl.ds(row + 1, rows)]
            lane = lane_of(c.shape)
            low = lane >= apart
            high = lane < LANES - apart
            zm = jnp.where(low, roll(c, apart, 1), 0.0)
            zp = jnp.where(high, roll(c, -apart, 1), 0.0)
            CX[i, at] = h * (c + xm)
            CY[i, at] = h * (c + ym)
            CM[i, at] = jnp.where(low, h * (c + zm), 0.0)
            CP[i, at] = jnp.where(high, h * (c + zp), 0.0)
            d = h * (6.0 * c + ((xm + xp) + (ym + yp) + (zm + zp)))
            D[i, at] = d
            x = g * nx + i - hx
            y = lax.broadcasted_iota(jnp.int32, c.shape, 0) + (b * ny + row - HY)
            inside = (y >= 0) & (y < B * ny) & (x >= 0) & (x < G * nx)
            Q[i, at] = jnp.where(inside, W / d, 0.0)
            return carry

        lax.fori_loop(first, last, plane, 0)

    def across(level, V, CX, CY, CM, CP, i, row, rows):
        apart = 1 << level
        at = pl.ds(row, rows)
        up = pl.ds(row + 1, rows)
        v = V[i, at]
        total = CX[i, at] * V[i - 1, at] + CX[i + 1, at] * V[i + 1, at]
        total = total + (CY[i, at] * V[i, pl.ds(row - 1, rows)] + CY[i, up] * V[i, up])
        total = total + (CM[i, at] * roll(v, apart, 1) + CP[i, at] * roll(v, -apart, 1))
        return v, total

    def first_sweep(V, Q, S, first, last, row, rows):
        def plane(i, carry):
            V[i, pl.ds(row, rows)] = Q[i, pl.ds(row, rows)] * S[i, pl.ds(row, rows)]
            return carry

        lax.fori_loop(first, last, plane, 0)

    def sweep(level, V, U, S, Q, coeffs, first, last, row, rows, drop_x=0, drop_y=0):
        def plane(i, carry):
            v, total = across(level, V, *coeffs, i, row, rows)
            U[i - drop_x, pl.ds(row - drop_y, rows)] = (1.0 - W) * v + Q[i, pl.ds(row, rows)] * (
                S[i, pl.ds(row, rows)] + total
            )
            return carry

        lax.fori_loop(first, last, plane, 0)

    def residual(level, V, S, D, coeffs, i, row, rows):
        v, total = across(level, V, *coeffs, i, row, rows)
        return S[i, pl.ds(row, rows)] - (D[i, pl.ds(row, rows)] * v - total)

    coeffs0 = (CX0, CY0, CM0, CP0)
    coeffs1 = (CX1, CY1, CM1, CP1)
    row0, rows0 = 4, 40
    row1, rows1 = 4, 24

    recv_all(beta_halo)
    setup(0, B0, CX0, CY0, CM0, CP0, Q0, D0, 1, 23, row0, rows0, H0, X0, Y0)
    load_s.wait()
    recv_all(source_halo)
    first_sweep(V0, Q0, S0, 1, 23, row0, rows0)
    sweep(0, V0, U0, S0, Q0, coeffs0, 2, 22, row0, rows0)

    def down0(p, carry):
        i = H0 + 2 * p
        pair = residual(0, U0, S0, D0, coeffs0, i, HY, Y0) + residual(0, U0, S0, D0, coeffs0, i + 1, HY, Y0)
        S1[H1 + p, pl.ds(HY, Y0 // 2)] = halve(pair, 1, p)
        return carry

    lax.fori_loop(0, X0 // 2, down0, 0)
    source1_halo = halo_copies(3, S1, S1, X0 // 2, H1, Y0 // 2, False)
    start_all(source1_halo)

    recv_all(beta1_halo)
    setup(1, B1, CX1, CY1, CM1, CP1, Q1, D1, 1, 17, row1, rows1, H1, X0 // 2, Y0 // 2)
    recv_all(source1_halo)
    first_sweep(V1, Q1, S1, 1, 17, row1, rows1)
    sweep(1, V1, U1, S1, Q1, coeffs1, 2, 16, row1, rows1)
    planes = []
    for p in range(X0 // 4):
        i = H1 + 2 * p
        pair = residual(1, U1, S1, D1, coeffs1, i, HY, Y0 // 2) + residual(1, U1, S1, D1, coeffs1, i + 1, HY, Y0 // 2)
        planes.append(halve(pair, 2, p))
    PS[...] = pack(planes)
    gather_start(1, PS, GS)

    def neighbours(v, level):
        st, zs = 1 << (level - 2), 1 << level
        before = [v[i - 1] for i in range(G)]
        after = [v[(i + 1) % G] for i in range(G)]
        if st == 4:
            xm, xp = before, after
        else:
            k = lane_of(v[0].shape) & 3
            xm = [jnp.where(k >= st, roll(v[i], st, 1), roll(before[i], st - 4, 1)) for i in range(G)]
            xp = [jnp.where(k < 4 - st, roll(v[i], -st, 1), roll(after[i], 4 - st, 1)) for i in range(G)]
        ym = [roll(a, 1, 0) for a in v]
        yp = [roll(a, -1, 0) for a in v]
        zm = [roll(a, zs, 1) for a in v]
        zp = [roll(a, -zs, 1) for a in v]
        return xm, xp, ym, yp, zm, zp

    def setup_whole(beta, C, level):
        st, zs = 1 << (level - 2), 1 << level
        h = 0.5 * 0.25**level
        near = neighbours(beta, level)
        shape = beta[0].shape
        lane = lane_of(shape)
        row = lax.broadcasted_iota(jnp.int32, shape, 0)
        for i in range(G):
            ok = [
                ((lane & 3) >= st) if i == 0 else None,
                ((lane & 3) < 4 - st) if i == G - 1 else None,
                row > 0,
                row < shape[0] - 1,
                lane >= zs,
                lane < LANES - zs,
            ]
            total = 6.0 * beta[i]
            for d in range(6):
                there = near[d][i] if ok[d] is None else jnp.where(ok[d], near[d][i], 0.0)
                total = total + there
                face = h * (beta[i] + there)
                C[d, i] = face if ok[d] is None else jnp.where(ok[d], face, 0.0)
            diag = h * total
            C[6, i] = diag
            C[7, i] = W / diag

    def sum_across(v, C, level):
        near = neighbours(v, level)
        out = []
        for i in range(G):
            out.append(
                (C[0, i] * near[0][i] + C[1, i] * near[1][i])
                + (C[2, i] * near[2][i] + C[3, i] * near[3][i])
                + (C[4, i] * near[4][i] + C[5, i] * near[5][i])
            )
        return out

    def sweep_whole(v, s, C, level):
        total = sum_across(v, C, level)
        return [(1.0 - W) * v[i] + C[7, i] * (s[i] + total[i]) for i in range(G)]

    def coarsen(v, level):
        st, zs = 1 << (level - 2), 1 << level
        rows = v[0].shape[0]
        out = []
        for i in range(G):
            E[i, pl.ds(0, rows)] = pair_lanes(pair_lanes(v[i], st), zs)
            out.append(0.125 * (E[i, pl.ds(0, rows // 2, stride=2)] + E[i, pl.ds(1, rows // 2, stride=2)]))
        return out

    def refine(v):
        rows = v[0].shape[0]
        out = []
        for i in range(G):
            E[i, pl.ds(0, rows, stride=2)] = v[i]
            E[i, pl.ds(1, rows, stride=2)] = v[i]
            out.append(E[i, pl.ds(0, 2 * rows)])
        return out

    gather_recv(0, GB)
    beta2 = [GB[i] for i in range(G)]
    setup_whole(beta2, C2, 2)
    beta3 = coarsen(beta2, 2)
    setup_whole(beta3, C3, 3)
    beta4 = coarsen(beta3, 3)
    setup_whole(beta4, C4, 4)

    gather_recv(1, GS)
    s2 = [GS[i] for i in range(G)]
    v = [C2[7, i] * s2[i] for i in range(G)]
    v = sweep_whole(v, s2, C2, 2)
    for i in range(G):
        V2[i + 1, pl.ds(8, ry2)] = v[i]
    total = sum_across(v, C2, 2)
    s3 = coarsen([s2[i] - (C2[6, i] * v[i] - total[i]) for i in range(G)], 2)
    v = [C3[7, i] * s3[i] for i in range(G)]
    v = sweep_whole(v, s3, C3, 3)
    for i in range(G):
        F3[0, i] = v[i]
        F3[1, i] = s3[i]
    total = sum_across(v, C3, 3)
    s4 = coarsen([s3[i] - (C3[6, i] * v[i] - total[i]) for i in range(G)], 3)

    def dot(a, c):
        acc = a[0] * c[0]
        for i in range(1, G):
            acc = acc + a[i] * c[i]
        part = acc[0:8]
        for j in range(8, ry4, 8):
            part = part + acc[j : j + 8]
        return jnp.sum(jnp.sum(part, axis=0, keepdims=True), axis=1, keepdims=True)

    def cg(step, carry):
        x, r, p, rr = carry
        near = sum_across(p, C4, 4)
        q = [C4[6, i] * p[i] - near[i] for i in range(G)]
        alpha = rr / dot(p, q)
        x = [x[i] + alpha * p[i] for i in range(G)]
        r = [r[i] - alpha * q[i] for i in range(G)]
        new = dot(r, r)
        ratio = new / rr
        p = [r[i] + ratio * p[i] for i in range(G)]
        return x, r, p, new

    zero = [jnp.zeros((ry4, LANES), F32) for i in range(G)]
    x4 = lax.fori_loop(0, COARSE, cg, (zero, s4, s4, dot(s4, s4)))[0]

    up = refine(x4)
    s3 = [F3[1, i] for i in range(G)]
    v = [F3[0, i] + up[i] for i in range(G)]
    for _ in range(SWEEPS):
        v = sweep_whole(v, s3, C3, 3)
    up = refine(v)
    s2 = [GS[i] for i in range(G)]
    v = [V2[i + 1, pl.ds(8, ry2)] + up[i] for i in range(G)]
    for _ in range(SWEEPS):
        v = sweep_whole(v, s2, C2, 2)
    for i in range(G):
        V2[i + 1, pl.ds(8, ry2)] = v[i]

    for x2 in range(-2, 6):
        k = x2 % 4
        window = V2[g + 1 + x2 // 4, pl.ds(pl.multiple_of(b * 8, 8), 24)]
        one = jnp.where((lane_of(window.shape) & 3) == k, window, 0.0)
        one = one + roll(one, 1 if k in (0, 2) else -1, 1)
        one = one + roll(one, 2 if k in (0, 1) else -2, 1)
        T[x2 + 2, pl.ds(0, 24)] = one
    for x2 in range(-2, 6):
        add = T[x2 + 2, pl.ds(6, 12)]
        for i in (2 * x2 + 5, 2 * x2 + 6):
            if 2 <= i < 16:
                for odd in (0, 1):
                    at = pl.ds(row1 + odd, 12, stride=2)
                    U1[i, at] = U1[i, at] + add
    sweep(1, U1, V1, S1, Q1, coeffs1, 3, 15, row1, rows1)
    sweep(1, V1, U1, S1, Q1, coeffs1, 4, 14, row1, rows1)

    def prolong0(i, carry):
        add = U1[i + 3, pl.ds(6, 20)]
        for half in (0, 1):
            for odd in (0, 1):
                at = pl.ds(row0 + odd, 20, stride=2)
                U0[2 * i + half, at] = U0[2 * i + half, at] + add
        return carry

    lax.fori_loop(1, 11, prolong0, 0)
    sweep(0, U0, V0, S0, Q0, coeffs0, 3, 21, row0, rows0)
    sweep(0, V0, out_ref, S0, Q0, coeffs0, 4, 20, HY, Y0, H0, HY)

    sent_all(beta_halo)
    sent_all(source_halo)
    sent_all(beta1_halo)
    sent_all(source1_halo)
    gather_sent(0, PB)
    gather_sent(1, PS)


def in_one_kernel(G, B, right_side, beta):
    level0 = pltpu.VMEM((X0 + 2 * H0, Y0 + 2 * HY, LANES), F32)
    level1 = pltpu.VMEM((X0 // 2 + 2 * H1, Y0 // 2 + 2 * HY, LANES), F32)
    return pl.pallas_call(
        functools.partial(kernel, G, B),
        out_shape=jax.ShapeDtypeStruct(right_side.shape, F32),
        in_specs=[pl.BlockSpec(memory_space=pl.ANY)] * 2,
        out_specs=pl.BlockSpec(memory_space=pltpu.VMEM),
        scratch_shapes=[level0] * 10
        + [level1] * 10
        + [
            pltpu.VMEM((8, Y0, LANES), F32),
            pltpu.VMEM((8, LANES), F32),
            pltpu.VMEM((8, LANES), F32),
            pltpu.VMEM((G, 8 * B, LANES), F32),
            pltpu.VMEM((G, 8 * B, LANES), F32),
            pltpu.VMEM((G + 2, 8 * B + 16, LANES), F32),
            pltpu.VMEM((8, G, 8 * B, LANES), F32),
            pltpu.VMEM((8, G, 4 * B, LANES), F32),
            pltpu.VMEM((8, G, 2 * B, LANES), F32),
            pltpu.VMEM((G, 8 * B, LANES), F32),
            pltpu.VMEM((2, G, 4 * B, LANES), F32),
            pltpu.SemaphoreType.DMA((4, 8)),
            pltpu.SemaphoreType.DMA((4, 8)),
            pltpu.SemaphoreType.DMA((2, G * B)),
            pltpu.SemaphoreType.DMA((2,)),
            pltpu.SemaphoreType.DMA((1,)),
            pltpu.SemaphoreType.DMA((2,)),
        ],
        compiler_params=pltpu.CompilerParams(
            collective_id=0, has_side_effects=True, vmem_limit_bytes=40 * 1024 * 1024
        ),
    )(right_side, beta)


relax_weight = 2.0 / 3.0


def with_halo(shard, sides, width):
    for axis, dim in sides:
        size, length = (lax.axis_size(axis), shard.shape[dim])
        up = [(i, (i + 1) % size) for i in range(size - 1)]
        down = [(j, i) for i, j in up]
        last = lax.slice_in_dim(shard, length - width, length, axis=dim)
        leading = lax.slice_in_dim(shard, 0, width, axis=dim)
        before = lax.ppermute(last, axis, up)
        after = lax.ppermute(leading, axis, down)
        shard = jnp.concatenate([before, shard, after], axis=dim)
    return shard


def from_partner(block, axis, apart):
    count = lax.axis_size(axis)
    route = []
    for low in range(count):
        high = low | 1 << apart
        if high != low and high < count:
            route += [(low, high), (high, low)]
    return lax.ppermute(block, axis, route)


def pad_zeros(field):
    return jnp.pad(field, 1)


def pad_local(field):
    extended = with_halo(field, (("grp", 0), ("box", 1)), 1)
    return jnp.pad(extended, ((0, 0), (0, 0), (1, 1)))


def face_coeffs(padded_beta):
    face_x = 0.5 * (padded_beta[1:, 1:-1, 1:-1] + padded_beta[:-1, 1:-1, 1:-1])
    face_y = 0.5 * (padded_beta[1:-1, 1:, 1:-1] + padded_beta[1:-1, :-1, 1:-1])
    face_z = 0.5 * (padded_beta[1:-1, 1:-1, 1:] + padded_beta[1:-1, 1:-1, :-1])
    return (face_x, face_y, face_z)


def inverse_diagonal(coeffs, scale):
    face_x, face_y, face_z = coeffs
    total = (
        face_x[:-1]
        + face_x[1:]
        + face_y[:, :-1]
        + face_y[:, 1:]
        + face_z[:, :, :-1]
        + face_z[:, :, 1:]
    )
    return 1.0 / (scale * total)


def apply_operator(padded, coeffs, scale):
    face_x, face_y, face_z = coeffs
    centre = padded[1:-1, 1:-1, 1:-1]
    total = face_x[:-1] * (centre - padded[:-2, 1:-1, 1:-1]) + face_x[1:] * (
        centre - padded[2:, 1:-1, 1:-1]
    )
    total = (
        total
        + face_y[:, :-1] * (centre - padded[1:-1, :-2, 1:-1])
        + face_y[:, 1:] * (centre - padded[1:-1, 2:, 1:-1])
    )
    total = (
        total
        + face_z[:, :, :-1] * (centre - padded[1:-1, 1:-1, :-2])
        + face_z[:, :, 1:] * (centre - padded[1:-1, 1:-1, 2:])
    )
    return scale * total


def jacobi_sweeps(field, source, coeffs, inverse, scale, count, padder):
    for sweep_index in range(count):
        field = (
            field + relax_weight * (source - apply_operator(padder(field), coeffs, scale)) * inverse
        )
    return field


def conjugate_solve(source, coeffs, scale, count):
    field = jnp.zeros_like(source)
    remain = source
    direction = source
    norm_now = jnp.sum(remain * remain)
    for step_index in range(count):
        image = apply_operator(pad_zeros(direction), coeffs, scale)
        alpha = norm_now / jnp.sum(direction * image)
        field = field + alpha * direction
        remain = remain - alpha * image
        norm_next = jnp.sum(remain * remain)
        direction = remain + norm_next / norm_now * direction
        norm_now = norm_next
    return field


def restrict_mean(field):
    size_a, size_b, size_c = field.shape
    blocks = field.reshape(size_a // 2, 2, size_b // 2, 2, size_c // 2, 2)
    return jnp.mean(blocks, axis=(1, 3, 5))


def prolong_copy(field):
    return jnp.repeat(jnp.repeat(jnp.repeat(field, 2, axis=0), 2, axis=1), 2, axis=2)


def merge_groups(pieces):
    group_index = lax.axis_index("grp")
    for bit_index in range(lax.axis_size("grp").bit_length() - 1):
        partner = from_partner(pieces, "grp", bit_index)
        upper = group_index >> bit_index & 1 == 1
        pieces = tuple(
            (
                jnp.where(
                    upper,
                    jnp.concatenate([theirs, own_piece], 0),
                    jnp.concatenate([own_piece, theirs], 0),
                )
                for own_piece, theirs in zip(pieces, partner)
            )
        )
    return pieces


def merge_boxes(pieces):
    return lax.all_gather(pieces, "box", axis=1, tiled=True)


def shards(right_side, beta):
    source = right_side
    level_beta = beta
    saved = []
    for level in range(LEVELS):
        scale = 0.25**level
        coeffs = face_coeffs(pad_local(level_beta))
        inverse = inverse_diagonal(coeffs, scale)
        field = relax_weight * source * inverse
        field = jacobi_sweeps(field, source, coeffs, inverse, scale, SWEEPS - 1, pad_local)
        residual = source - apply_operator(pad_local(field), coeffs, scale)
        saved.append((field, source, coeffs, inverse, scale))
        source = restrict_mean(residual)
        level_beta = restrict_mean(level_beta)
    low_scale = 0.25**LEVELS
    whole_source, whole_beta = merge_boxes(merge_groups((source, level_beta)))
    low_coeffs = face_coeffs(pad_zeros(whole_beta))
    whole_field = conjugate_solve(whole_source, low_coeffs, low_scale, COARSE)
    block_a, block_b, block_c = source.shape
    field = lax.dynamic_slice(
        whole_field,
        (lax.axis_index("grp") * block_a, lax.axis_index("box") * block_b, 0),
        (block_a, block_b, block_c),
    )
    for level in range(LEVELS - 1, -1, -1):
        kept, level_source, coeffs, inverse, scale = saved[level]
        field = kept + prolong_copy(field)
        field = jacobi_sweeps(field, level_source, coeffs, inverse, scale, SWEEPS, pad_local)
    return field


def solution(mesh):
    placed = P("grp", "box", None)
    G, B = mesh.shape["grp"], mesh.shape["box"]
    small = G * B <= 64 and (2 * B) % 8 == 0 and G > 1

    def local(right_side, beta):
        if small and right_side.shape == (X0, Y0, LANES):
            return in_one_kernel(G, B, right_side, beta)
        return shards(right_side, beta)

    return jax.shard_map(local, mesh=mesh, in_specs=(placed, placed), out_specs=placed, check_vma=False)
```

```python
import functools

import jax
import jax.numpy as jnp
from jax import lax
from jax.experimental import pallas as pl
from jax.experimental.pallas import tpu as pltpu
from jax.sharding import PartitionSpec as P

LEVELS = 4
SWEEPS = 2
COARSE = 8
W = 2.0 / 3.0
MESH = pl.DeviceIdType.MESH
F32 = jnp.float32

X0, Y0, LANES = 16, 32, 128
H0 = 4
H1 = 5
HY = 8
DIRS = [(dx, dy) for dx in (-1, 0, 1) for dy in (-1, 0, 1) if (dx, dy) != (0, 0)]


def roll(v, shift, axis):
    return pltpu.roll(v, shift % v.shape[axis], axis)


def lane_of(shape):
    return lax.broadcasted_iota(jnp.int32, shape, len(shape) - 1)


def pair_lanes(v, apart):
    lane = lane_of(v.shape)
    return v + jnp.where((lane & apart) == 0, roll(v, -apart, 1), roll(v, apart, 1))


def span(size, halo, step, own):
    if step == 0:
        return (halo, size), (halo, size)
    if step < 0:
        return (halo, own), (halo + size, own)
    return (halo + size - own, own), (halo - own, own)


def kernel(
    G, B, rs_ref, be_ref, out_ref,
    B0, S0, V0, U0, CX0, CY0, CM0, CP0, Q0, D0,
    B1, S1, V1, U1, CX1, CY1, CM1, CP1, Q1, D1,
    T, PB, PS, GB, GS, V2, C2, C3, C4, E, F3,
    halo_send, halo_recv, ga_send, ga_recv, own_sem, loc_sem,
):
    n = G * B
    g = lax.axis_index("grp")
    b = lax.axis_index("box")
    me = g * B + b
    ry2, ry3, ry4 = 8 * B, 4 * B, 2 * B

    own0 = (pl.ds(H0, X0), pl.ds(HY, Y0))
    load_b = pltpu.make_async_copy(be_ref, B0.at[own0[0], own0[1]], loc_sem.at[0])
    load_s = pltpu.make_async_copy(rs_ref, S0.at[own0[0], own0[1]], loc_sem.at[1])
    load_b.start()
    load_s.start()

    barrier = pltpu.get_barrier_semaphore()

    def greet(d, carry):
        peer = (me + d) % n
        pl.semaphore_signal(barrier, inc=1, device_id=(peer // B, peer % B), device_id_type=MESH)
        return carry

    lax.fori_loop(1, n, greet, 0)

    for ref, nx, hx, ny in ((B0, X0, H0, Y0), (S0, X0, H0, Y0), (B1, X0 // 2, H1, Y0 // 2), (S1, X0 // 2, H1, Y0 // 2)):
        rows = ny + 2 * HY
        planes = nx + 2 * hx

        @pl.when(g == 0)
        def _():
            ref[pl.ds(0, hx)] = jnp.zeros((hx, rows, LANES), F32)

        @pl.when(g == G - 1)
        def _():
            ref[pl.ds(hx + nx, hx)] = jnp.zeros((hx, rows, LANES), F32)

        @pl.when(b == 0)
        def _():
            ref[:, pl.ds(0, HY)] = jnp.zeros((planes, HY, LANES), F32)

        @pl.when(b == B - 1)
        def _():
            ref[:, pl.ds(HY + ny, HY)] = jnp.zeros((planes, HY, LANES), F32)

    V2[0] = jnp.zeros((ry2 + 16, LANES), F32)
    V2[G + 1] = jnp.zeros((ry2 + 16, LANES), F32)
    V2[:, pl.ds(0, 8)] = jnp.zeros((G + 2, 8, LANES), F32)
    V2[:, pl.ds(8 + ry2, 8)] = jnp.zeros((G + 2, 8, LANES), F32)

    pl.semaphore_wait(barrier, n - 1)

    def halo_copies(kind, src, dst, nx, hx, ny, deep, tall, src_is_input):
        made = []
        for at, (dx, dy) in enumerate(DIRS):
            (sx, lx), (tx, _) = span(nx, hx, dx, deep)
            (sy, ly), (ty, _) = span(ny, HY, dy, tall)
            if src_is_input:
                sx, sy = sx - hx, sy - HY
            copy = pltpu.make_async_remote_copy(
                src_ref=src.at[pl.ds(sx, lx), pl.ds(sy, ly)],
                dst_ref=dst.at[pl.ds(tx, lx), pl.ds(ty, ly)],
                send_sem=halo_send.at[kind, at],
                recv_sem=halo_recv.at[kind, at],
                device_id=(g + dx, b + dy),
                device_id_type=MESH,
            )
            there = (g + dx >= 0) & (g + dx < G) & (b + dy >= 0) & (b + dy < B)
            here = (g - dx >= 0) & (g - dx < G) & (b - dy >= 0) & (b - dy < B)
            made.append((copy, there, here))
        return made

    def start_all(copies):
        for copy, there, _ in copies:
            pl.when(there)(copy.start)

    def recv_all(copies):
        for copy, _, here in copies:
            pl.when(here)(copy.wait_recv)

    def sent_all(copies):
        for copy, there, _ in copies:
            pl.when(there)(copy.wait_send)

    def gather_start(which, packed, whole):
        pltpu.make_async_copy(packed, whole.at[g, pl.ds(pl.multiple_of(b * 8, 8), 8)], ga_recv.at[which]).start()

        def one(d, carry):
            peer = (me + d) % n
            pltpu.make_async_remote_copy(
                src_ref=packed,
                dst_ref=whole.at[g, pl.ds(pl.multiple_of(b * 8, 8), 8)],
                send_sem=ga_send.at[which, d],
                recv_sem=ga_recv.at[which],
                device_id=(peer // B, peer % B),
                device_id_type=MESH,
            ).start()
            return carry

        lax.fori_loop(1, n, one, 0)

    def gather_recv(which, whole):
        pltpu.make_async_copy(whole, whole, ga_recv.at[which]).wait()

    def gather_sent(which, packed):
        def one(d, carry):
            pltpu.make_async_copy(packed, packed, ga_send.at[which, d]).wait()
            return carry

        lax.fori_loop(1, n, one, 0)

    beta_halo = halo_copies(0, be_ref, B0, X0, H0, Y0, 4, 4, True)
    source_halo = halo_copies(1, rs_ref, S0, X0, H0, Y0, 3, 4, True)
    start_all(beta_halo)
    start_all(source_halo)
    load_b.wait()

    def halve(pair, apart, slot):
        rows = pair.shape[0]
        T[slot, pl.ds(0, rows)] = pair_lanes(pair, apart)
        return 0.125 * (T[slot, pl.ds(0, rows // 2, stride=2)] + T[slot, pl.ds(1, rows // 2, stride=2)])

    def pack(planes):
        lane = lane_of(planes[0].shape) & 3
        packed = planes[3]
        for k in (2, 1, 0):
            packed = jnp.where(lane == k, planes[k], packed)
        return packed

    for p in range(X0 // 2):
        B1[H1 + p, pl.ds(HY, Y0 // 2)] = halve(
            B0[H0 + 2 * p, pl.ds(HY, Y0)] + B0[H0 + 2 * p + 1, pl.ds(HY, Y0)], 1, p
        )
    beta1_halo = halo_copies(2, B1, B1, X0 // 2, H1, Y0 // 2, 5, 8, False)
    start_all(beta1_halo)
    PB[...] = pack([
        halve(B1[H1 + 2 * p, pl.ds(HY, Y0 // 2)] + B1[H1 + 2 * p + 1, pl.ds(HY, Y0 // 2)], 2, p)
        for p in range(X0 // 4)
    ])
    gather_start(0, PB, GB)

    def setup(level, Bl, CX, CY, CM, CP, Q, D, first, last, row, rows, hx, nx, ny):
        apart = 1 << level
        h = 0.5 * 0.25**level

        def plane(i, carry):
            at = pl.ds(row, rows)
            c = Bl[i, at]
            xm = Bl[i - 1, at]
            xp = Bl[i + 1, at]
            ym = Bl[i, pl.ds(row - 1, rows)]
            yp = Bl[i, pl.ds(row + 1, rows)]
            lane = lane_of(c.shape)
            low = lane >= apart
            high = lane < LANES - apart
            zm = jnp.where(low, roll(c, apart, 1), 0.0)
            zp = jnp.where(high, roll(c, -apart, 1), 0.0)
            CX[i, at] = h * (c + xm)
            CY[i, at] = h * (c + ym)
            CM[i, at] = jnp.where(low, h * (c + zm), 0.0)
            CP[i, at] = jnp.where(high, h * (c + zp), 0.0)
            d = h * (6.0 * c + ((xm + xp) + (ym + yp) + (zm + zp)))
            D[i, at] = d
            x = g * nx + i - hx
            y = lax.broadcasted_iota(jnp.int32, c.shape, 0) + (b * ny + row - HY)
            inside = (y >= 0) & (y < B * ny) & (x >= 0) & (x < G * nx)
            Q[i, at] = jnp.where(inside, W / d, 0.0)
            return carry

        lax.fori_loop(first, last, plane, 0, unroll=True)

    def across(level, V, CX, CY, CM, CP, i, row, rows):
        apart = 1 << level
        at = pl.ds(row, rows)
        up = pl.ds(row + 1, rows)
        v = V[i, at]
        total = CX[i, at] * V[i - 1, at] + CX[i + 1, at] * V[i + 1, at]
        total = total + (CY[i, at] * V[i, pl.ds(row - 1, rows)] + CY[i, up] * V[i, up])
        total = total + (CM[i, at] * roll(v, apart, 1) + CP[i, at] * roll(v, -apart, 1))
        return v, total

    def first_sweep(V, Q, S, first, last, row, rows):
        def plane(i, carry):
            V[i, pl.ds(row, rows)] = Q[i, pl.ds(row, rows)] * S[i, pl.ds(row, rows)]
            return carry

        lax.fori_loop(first, last, plane, 0, unroll=True)

    def sweep(level, V, U, S, Q, coeffs, first, last, row, rows, drop_x=0, drop_y=0):
        def plane(i, carry):
            v, total = across(level, V, *coeffs, i, row, rows)
            U[i - drop_x, pl.ds(row - drop_y, rows)] = (1.0 - W) * v + Q[i, pl.ds(row, rows)] * (
                S[i, pl.ds(row, rows)] + total
            )
            return carry

        lax.fori_loop(first, last, plane, 0, unroll=True)

    def residual(level, V, S, D, coeffs, i, row, rows):
        v, total = across(level, V, *coeffs, i, row, rows)
        return S[i, pl.ds(row, rows)] - (D[i, pl.ds(row, rows)] * v - total)

    coeffs0 = (CX0, CY0, CM0, CP0)
    coeffs1 = (CX1, CY1, CM1, CP1)
    row0, rows0 = 4, 40
    row1, rows1 = 4, 24

    recv_all(beta_halo)
    setup(0, B0, CX0, CY0, CM0, CP0, Q0, D0, 1, 23, row0, rows0, H0, X0, Y0)
    load_s.wait()
    recv_all(source_halo)
    first_sweep(V0, Q0, S0, 1, 23, row0, rows0)
    sweep(0, V0, U0, S0, Q0, coeffs0, 2, 22, row0, rows0)

    def down0(p, carry):
        i = H0 + 2 * p
        pair = residual(0, U0, S0, D0, coeffs0, i, HY, Y0) + residual(0, U0, S0, D0, coeffs0, i + 1, HY, Y0)
        S1[H1 + p, pl.ds(HY, Y0 // 2)] = halve(pair, 1, p)
        return carry

    lax.fori_loop(0, X0 // 2, down0, 0, unroll=True)
    source1_halo = halo_copies(3, S1, S1, X0 // 2, H1, Y0 // 2, 4, 4, False)
    start_all(source1_halo)

    recv_all(beta1_halo)
    setup(1, B1, CX1, CY1, CM1, CP1, Q1, D1, 1, 17, row1, rows1, H1, X0 // 2, Y0 // 2)
    recv_all(source1_halo)
    first_sweep(V1, Q1, S1, 1, 17, row1, rows1)
    sweep(1, V1, U1, S1, Q1, coeffs1, 2, 16, row1, rows1)
    planes = []
    for p in range(X0 // 4):
        i = H1 + 2 * p
        pair = residual(1, U1, S1, D1, coeffs1, i, HY, Y0 // 2) + residual(1, U1, S1, D1, coeffs1, i + 1, HY, Y0 // 2)
        planes.append(halve(pair, 2, p))
    PS[...] = pack(planes)
    gather_start(1, PS, GS)

    def neighbours(v, level):
        st, zs = 1 << (level - 2), 1 << level
        before = [v[i - 1] for i in range(G)]
        after = [v[(i + 1) % G] for i in range(G)]
        if st == 4:
            xm, xp = before, after
        else:
            k = lane_of(v[0].shape) & 3
            xm = [jnp.where(k >= st, roll(v[i], st, 1), roll(before[i], st - 4, 1)) for i in range(G)]
            xp = [jnp.where(k < 4 - st, roll(v[i], -st, 1), roll(after[i], 4 - st, 1)) for i in range(G)]
        ym = [roll(a, 1, 0) for a in v]
        yp = [roll(a, -1, 0) for a in v]
        zm = [roll(a, zs, 1) for a in v]
        zp = [roll(a, -zs, 1) for a in v]
        return xm, xp, ym, yp, zm, zp

    def setup_whole(beta, C, level):
        st, zs = 1 << (level - 2), 1 << level
        h = 0.5 * 0.25**level
        near = neighbours(beta, level)
        shape = beta[0].shape
        lane = lane_of(shape)
        row = lax.broadcasted_iota(jnp.int32, shape, 0)
        for i in range(G):
            ok = [
                ((lane & 3) >= st) if i == 0 else None,
                ((lane & 3) < 4 - st) if i == G - 1 else None,
                row > 0,
                row < shape[0] - 1,
                lane >= zs,
                lane < LANES - zs,
            ]
            total = 6.0 * beta[i]
            for d in range(6):
                there = near[d][i] if ok[d] is None else jnp.where(ok[d], near[d][i], 0.0)
                total = total + there
                face = h * (beta[i] + there)
                C[d, i] = face if ok[d] is None else jnp.where(ok[d], face, 0.0)
            diag = h * total
            C[6, i] = diag
            C[7, i] = W / diag

    def sum_across(v, C, level):
        near = neighbours(v, level)
        out = []
        for i in range(G):
            out.append(
                (C[0, i] * near[0][i] + C[1, i] * near[1][i])
                + (C[2, i] * near[2][i] + C[3, i] * near[3][i])
                + (C[4, i] * near[4][i] + C[5, i] * near[5][i])
            )
        return out

    def sweep_whole(v, s, C, level):
        total = sum_across(v, C, level)
        return [(1.0 - W) * v[i] + C[7, i] * (s[i] + total[i]) for i in range(G)]

    def coarsen(v, level):
        st, zs = 1 << (level - 2), 1 << level
        rows = v[0].shape[0]
        out = []
        for i in range(G):
            E[i, pl.ds(0, rows)] = pair_lanes(pair_lanes(v[i], st), zs)
            out.append(0.125 * (E[i, pl.ds(0, rows // 2, stride=2)] + E[i, pl.ds(1, rows // 2, stride=2)]))
        return out

    def refine(v):
        rows = v[0].shape[0]
        out = []
        for i in range(G):
            E[i, pl.ds(0, rows, stride=2)] = v[i]
            E[i, pl.ds(1, rows, stride=2)] = v[i]
            out.append(E[i, pl.ds(0, 2 * rows)])
        return out

    gather_recv(0, GB)
    beta2 = [GB[i] for i in range(G)]
    setup_whole(beta2, C2, 2)
    beta3 = coarsen(beta2, 2)
    setup_whole(beta3, C3, 3)
    beta4 = coarsen(beta3, 3)
    setup_whole(beta4, C4, 4)

    gather_recv(1, GS)
    s2 = [GS[i] for i in range(G)]
    v = [C2[7, i] * s2[i] for i in range(G)]
    v = sweep_whole(v, s2, C2, 2)
    for i in range(G):
        V2[i + 1, pl.ds(8, ry2)] = v[i]
    total = sum_across(v, C2, 2)
    s3 = coarsen([s2[i] - (C2[6, i] * v[i] - total[i]) for i in range(G)], 2)
    v = [C3[7, i] * s3[i] for i in range(G)]
    v = sweep_whole(v, s3, C3, 3)
    for i in range(G):
        F3[0, i] = v[i]
        F3[1, i] = s3[i]
    total = sum_across(v, C3, 3)
    s4 = coarsen([s3[i] - (C3[6, i] * v[i] - total[i]) for i in range(G)], 3)

    def dot(a, c):
        acc = a[0] * c[0]
        for i in range(1, G):
            acc = acc + a[i] * c[i]
        part = acc[0:8]
        for j in range(8, ry4, 8):
            part = part + acc[j : j + 8]
        return jnp.sum(jnp.sum(part, axis=0, keepdims=True), axis=1, keepdims=True)

    def cg(step, carry):
        x, r, p, rr = carry
        near = sum_across(p, C4, 4)
        q = [C4[6, i] * p[i] - near[i] for i in range(G)]
        alpha = rr / dot(p, q)
        x = [x[i] + alpha * p[i] for i in range(G)]
        r = [r[i] - alpha * q[i] for i in range(G)]
        new = dot(r, r)
        ratio = new / rr
        p = [r[i] + ratio * p[i] for i in range(G)]
        return x, r, p, new

    zero = [jnp.zeros((ry4, LANES), F32) for i in range(G)]
    x4 = lax.fori_loop(0, COARSE, cg, (zero, s4, s4, dot(s4, s4)))[0]

    up = refine(x4)
    s3 = [F3[1, i] for i in range(G)]
    v = [F3[0, i] + up[i] for i in range(G)]
    for _ in range(SWEEPS):
        v = sweep_whole(v, s3, C3, 3)
    up = refine(v)
    s2 = [GS[i] for i in range(G)]
    v = [V2[i + 1, pl.ds(8, ry2)] + up[i] for i in range(G)]
    for _ in range(SWEEPS):
        v = sweep_whole(v, s2, C2, 2)
    for i in range(G):
        V2[i + 1, pl.ds(8, ry2)] = v[i]

    for x2 in range(-2, 6):
        k = x2 % 4
        window = V2[g + 1 + x2 // 4, pl.ds(pl.multiple_of(b * 8, 8), 24)]
        one = jnp.where((lane_of(window.shape) & 3) == k, window, 0.0)
        one = one + roll(one, 1 if k in (0, 2) else -1, 1)
        one = one + roll(one, 2 if k in (0, 1) else -2, 1)
        T[x2 + 2, pl.ds(0, 24)] = one
    for x2 in range(-2, 6):
        add = T[x2 + 2, pl.ds(6, 12)]
        for i in (2 * x2 + 5, 2 * x2 + 6):
            if 2 <= i < 16:
                for odd in (0, 1):
                    at = pl.ds(row1 + odd, 12, stride=2)
                    U1[i, at] = U1[i, at] + add
    sweep(1, U1, V1, S1, Q1, coeffs1, 3, 15, row1, rows1)
    sweep(1, V1, U1, S1, Q1, coeffs1, 4, 14, row1, rows1)

    def prolong0(i, carry):
        add = U1[i + 3, pl.ds(6, 20)]
        for half in (0, 1):
            for odd in (0, 1):
                at = pl.ds(row0 + odd, 20, stride=2)
                U0[2 * i + half, at] = U0[2 * i + half, at] + add
        return carry

    lax.fori_loop(1, 11, prolong0, 0, unroll=True)
    sweep(0, U0, V0, S0, Q0, coeffs0, 3, 21, row0, rows0)
    sweep(0, V0, out_ref, S0, Q0, coeffs0, 4, 20, HY, Y0, H0, HY)

    sent_all(beta_halo)
    sent_all(source_halo)
    sent_all(beta1_halo)
    sent_all(source1_halo)
    gather_sent(0, PB)
    gather_sent(1, PS)


def in_one_kernel(G, B, right_side, beta):
    level0 = pltpu.VMEM((X0 + 2 * H0, Y0 + 2 * HY, LANES), F32)
    level1 = pltpu.VMEM((X0 // 2 + 2 * H1, Y0 // 2 + 2 * HY, LANES), F32)
    return pl.pallas_call(
        functools.partial(kernel, G, B),
        out_shape=jax.ShapeDtypeStruct(right_side.shape, F32),
        in_specs=[pl.BlockSpec(memory_space=pl.ANY)] * 2,
        out_specs=pl.BlockSpec(memory_space=pltpu.VMEM),
        scratch_shapes=[level0] * 10
        + [level1] * 10
        + [
            pltpu.VMEM((8, Y0, LANES), F32),
            pltpu.VMEM((8, LANES), F32),
            pltpu.VMEM((8, LANES), F32),
            pltpu.VMEM((G, 8 * B, LANES), F32),
            pltpu.VMEM((G, 8 * B, LANES), F32),
            pltpu.VMEM((G + 2, 8 * B + 16, LANES), F32),
            pltpu.VMEM((8, G, 8 * B, LANES), F32),
            pltpu.VMEM((8, G, 4 * B, LANES), F32),
            pltpu.VMEM((8, G, 2 * B, LANES), F32),
            pltpu.VMEM((G, 8 * B, LANES), F32),
            pltpu.VMEM((2, G, 4 * B, LANES), F32),
            pltpu.SemaphoreType.DMA((4, 8)),
            pltpu.SemaphoreType.DMA((4, 8)),
            pltpu.SemaphoreType.DMA((2, G * B)),
            pltpu.SemaphoreType.DMA((2,)),
            pltpu.SemaphoreType.DMA((1,)),
            pltpu.SemaphoreType.DMA((2,)),
        ],
        compiler_params=pltpu.CompilerParams(
            collective_id=0, has_side_effects=True, vmem_limit_bytes=40 * 1024 * 1024
        ),
    )(right_side, beta)


relax_weight = 2.0 / 3.0


def with_halo(shard, sides, width):
    for axis, dim in sides:
        size, length = (lax.axis_size(axis), shard.shape[dim])
        up = [(i, (i + 1) % size) for i in range(size - 1)]
        down = [(j, i) for i, j in up]
        last = lax.slice_in_dim(shard, length - width, length, axis=dim)
        leading = lax.slice_in_dim(shard, 0, width, axis=dim)
        before = lax.ppermute(last, axis, up)
        after = lax.ppermute(leading, axis, down)
        shard = jnp.concatenate([before, shard, after], axis=dim)
    return shard


def from_partner(block, axis, apart):
    count = lax.axis_size(axis)
    route = []
    for low in range(count):
        high = low | 1 << apart
        if high != low and high < count:
            route += [(low, high), (high, low)]
    return lax.ppermute(block, axis, route)


def pad_zeros(field):
    return jnp.pad(field, 1)


def pad_local(field):
    extended = with_halo(field, (("grp", 0), ("box", 1)), 1)
    return jnp.pad(extended, ((0, 0), (0, 0), (1, 1)))


def face_coeffs(padded_beta):
    face_x = 0.5 * (padded_beta[1:, 1:-1, 1:-1] + padded_beta[:-1, 1:-1, 1:-1])
    face_y = 0.5 * (padded_beta[1:-1, 1:, 1:-1] + padded_beta[1:-1, :-1, 1:-1])
    face_z = 0.5 * (padded_beta[1:-1, 1:-1, 1:] + padded_beta[1:-1, 1:-1, :-1])
    return (face_x, face_y, face_z)


def inverse_diagonal(coeffs, scale):
    face_x, face_y, face_z = coeffs
    total = (
        face_x[:-1]
        + face_x[1:]
        + face_y[:, :-1]
        + face_y[:, 1:]
        + face_z[:, :, :-1]
        + face_z[:, :, 1:]
    )
    return 1.0 / (scale * total)


def apply_operator(padded, coeffs, scale):
    face_x, face_y, face_z = coeffs
    centre = padded[1:-1, 1:-1, 1:-1]
    total = face_x[:-1] * (centre - padded[:-2, 1:-1, 1:-1]) + face_x[1:] * (
        centre - padded[2:, 1:-1, 1:-1]
    )
    total = (
        total
        + face_y[:, :-1] * (centre - padded[1:-1, :-2, 1:-1])
        + face_y[:, 1:] * (centre - padded[1:-1, 2:, 1:-1])
    )
    total = (
        total
        + face_z[:, :, :-1] * (centre - padded[1:-1, 1:-1, :-2])
        + face_z[:, :, 1:] * (centre - padded[1:-1, 1:-1, 2:])
    )
    return scale * total


def jacobi_sweeps(field, source, coeffs, inverse, scale, count, padder):
    for sweep_index in range(count):
        field = (
            field + relax_weight * (source - apply_operator(padder(field), coeffs, scale)) * inverse
        )
    return field


def conjugate_solve(source, coeffs, scale, count):
    field = jnp.zeros_like(source)
    remain = source
    direction = source
    norm_now = jnp.sum(remain * remain)
    for step_index in range(count):
        image = apply_operator(pad_zeros(direction), coeffs, scale)
        alpha = norm_now / jnp.sum(direction * image)
        field = field + alpha * direction
        remain = remain - alpha * image
        norm_next = jnp.sum(remain * remain)
        direction = remain + norm_next / norm_now * direction
        norm_now = norm_next
    return field


def restrict_mean(field):
    size_a, size_b, size_c = field.shape
    blocks = field.reshape(size_a // 2, 2, size_b // 2, 2, size_c // 2, 2)
    return jnp.mean(blocks, axis=(1, 3, 5))


def prolong_copy(field):
    return jnp.repeat(jnp.repeat(jnp.repeat(field, 2, axis=0), 2, axis=1), 2, axis=2)


def merge_groups(pieces):
    group_index = lax.axis_index("grp")
    for bit_index in range(lax.axis_size("grp").bit_length() - 1):
        partner = from_partner(pieces, "grp", bit_index)
        upper = group_index >> bit_index & 1 == 1
        pieces = tuple(
            (
                jnp.where(
                    upper,
                    jnp.concatenate([theirs, own_piece], 0),
                    jnp.concatenate([own_piece, theirs], 0),
                )
                for own_piece, theirs in zip(pieces, partner)
            )
        )
    return pieces


def merge_boxes(pieces):
    return lax.all_gather(pieces, "box", axis=1, tiled=True)


def shards(right_side, beta):
    source = right_side
    level_beta = beta
    saved = []
    for level in range(LEVELS):
        scale = 0.25**level
        coeffs = face_coeffs(pad_local(level_beta))
        inverse = inverse_diagonal(coeffs, scale)
        field = relax_weight * source * inverse
        field = jacobi_sweeps(field, source, coeffs, inverse, scale, SWEEPS - 1, pad_local)
        residual = source - apply_operator(pad_local(field), coeffs, scale)
        saved.append((field, source, coeffs, inverse, scale))
        source = restrict_mean(residual)
        level_beta = restrict_mean(level_beta)
    low_scale = 0.25**LEVELS
    whole_source, whole_beta = merge_boxes(merge_groups((source, level_beta)))
    low_coeffs = face_coeffs(pad_zeros(whole_beta))
    whole_field = conjugate_solve(whole_source, low_coeffs, low_scale, COARSE)
    block_a, block_b, block_c = source.shape
    field = lax.dynamic_slice(
        whole_field,
        (lax.axis_index("grp") * block_a, lax.axis_index("box") * block_b, 0),
        (block_a, block_b, block_c),
    )
    for level in range(LEVELS - 1, -1, -1):
        kept, level_source, coeffs, inverse, scale = saved[level]
        field = kept + prolong_copy(field)
        field = jacobi_sweeps(field, level_source, coeffs, inverse, scale, SWEEPS, pad_local)
    return field


def solution(mesh):
    placed = P("grp", "box", None)
    G, B = mesh.shape["grp"], mesh.shape["box"]
    small = G * B <= 64 and (2 * B) % 8 == 0 and G > 1

    def local(right_side, beta):
        if small and right_side.shape == (X0, Y0, LANES):
            return in_one_kernel(G, B, right_side, beta)
        return shards(right_side, beta)

    return jax.shard_map(local, mesh=mesh, in_specs=(placed, placed), out_specs=placed, check_vma=False)
```

```python
import functools

import jax
import jax.numpy as jnp
from jax import lax
from jax.experimental import pallas as pl
from jax.experimental.pallas import tpu as pltpu
from jax.sharding import PartitionSpec as P

LEVELS = 4
SWEEPS = 2
COARSE = 8
W = 2.0 / 3.0
MESH = pl.DeviceIdType.MESH
F32 = jnp.float32

X0, Y0, LANES = 16, 32, 128
H0 = 4
H1 = 5
HY = 8
DIRS = [(dx, dy) for dx in (-1, 0, 1) for dy in (-1, 0, 1) if (dx, dy) != (0, 0)]


def roll(v, shift, axis):
    return pltpu.roll(v, shift % v.shape[axis], axis)


def lane_of(shape):
    return lax.broadcasted_iota(jnp.int32, shape, len(shape) - 1)


def pair_lanes(v, apart):
    lane = lane_of(v.shape)
    return v + jnp.where((lane & apart) == 0, roll(v, -apart, 1), roll(v, apart, 1))


def span(size, halo, step, own):
    if step == 0:
        return (halo, size), (halo, size)
    if step < 0:
        return (halo, own), (halo + size, own)
    return (halo + size - own, own), (halo - own, own)


def kernel(
    G, B, rs_ref, be_ref, out_ref,
    B0, S0, V0, U0, CX0, CY0, CM0, CP0, Q0, D0,
    B1, S1, V1, U1, CX1, CY1, CM1, CP1, Q1, D1,
    T, PB, PS, GB, GS, V2, C2, C3, C4, E, F3,
    halo_send, halo_recv, ga_send, ga_recv, own_sem, loc_sem,
):
    n = G * B
    g = lax.axis_index("grp")
    b = lax.axis_index("box")
    me = g * B + b
    ry2, ry3, ry4 = 8 * B, 4 * B, 2 * B

    own0 = (pl.ds(H0, X0), pl.ds(HY, Y0))
    load_b = pltpu.make_async_copy(be_ref, B0.at[own0[0], own0[1]], loc_sem.at[0])
    load_s = pltpu.make_async_copy(rs_ref, S0.at[own0[0], own0[1]], loc_sem.at[1])
    load_b.start()
    load_s.start()

    barrier = pltpu.get_barrier_semaphore()

    def greet(d, carry):
        peer = (me + d) % n
        pl.semaphore_signal(barrier, inc=1, device_id=(peer // B, peer % B), device_id_type=MESH)
        return carry

    lax.fori_loop(1, n, greet, 0)

    for ref, nx, hx, ny in ((B0, X0, H0, Y0), (S0, X0, H0, Y0), (B1, X0 // 2, H1, Y0 // 2), (S1, X0 // 2, H1, Y0 // 2)):
        rows = ny + 2 * HY
        planes = nx + 2 * hx

        @pl.when(g == 0)
        def _():
            ref[pl.ds(0, hx)] = jnp.zeros((hx, rows, LANES), F32)

        @pl.when(g == G - 1)
        def _():
            ref[pl.ds(hx + nx, hx)] = jnp.zeros((hx, rows, LANES), F32)

        @pl.when(b == 0)
        def _():
            ref[:, pl.ds(0, HY)] = jnp.zeros((planes, HY, LANES), F32)

        @pl.when(b == B - 1)
        def _():
            ref[:, pl.ds(HY + ny, HY)] = jnp.zeros((planes, HY, LANES), F32)

    V2[0] = jnp.zeros((ry2 + 16, LANES), F32)
    V2[G + 1] = jnp.zeros((ry2 + 16, LANES), F32)
    V2[:, pl.ds(0, 8)] = jnp.zeros((G + 2, 8, LANES), F32)
    V2[:, pl.ds(8 + ry2, 8)] = jnp.zeros((G + 2, 8, LANES), F32)

    pl.semaphore_wait(barrier, n - 1)

    def halo_copies(kind, src, dst, nx, hx, ny, deep, corner, tall, src_is_input):
        made = []
        for at, (dx, dy) in enumerate(DIRS):
            (sx, lx), (tx, _) = span(nx, hx, dx, deep if dy == 0 else corner)
            (sy, ly), (ty, _) = span(ny, HY, dy, tall)
            if src_is_input:
                sx, sy = sx - hx, sy - HY
            copy = pltpu.make_async_remote_copy(
                src_ref=src.at[pl.ds(sx, lx), pl.ds(sy, ly)],
                dst_ref=dst.at[pl.ds(tx, lx), pl.ds(ty, ly)],
                send_sem=halo_send.at[kind, at],
                recv_sem=halo_recv.at[kind, at],
                device_id=(g + dx, b + dy),
                device_id_type=MESH,
            )
            there = (g + dx >= 0) & (g + dx < G) & (b + dy >= 0) & (b + dy < B)
            here = (g - dx >= 0) & (g - dx < G) & (b - dy >= 0) & (b - dy < B)
            made.append((copy, there, here))
        return made

    def start_all(copies):
        for copy, there, _ in copies:
            pl.when(there)(copy.start)

    def recv_all(copies):
        for copy, _, here in copies:
            pl.when(here)(copy.wait_recv)

    def sent_all(copies):
        for copy, there, _ in copies:
            pl.when(there)(copy.wait_send)

    def gather_start(which, packed, whole):
        pltpu.make_async_copy(packed, whole.at[g, pl.ds(pl.multiple_of(b * 8, 8), 8)], ga_recv.at[which]).start()

        def one(d, carry):
            peer = (me + d) % n
            pltpu.make_async_remote_copy(
                src_ref=packed,
                dst_ref=whole.at[g, pl.ds(pl.multiple_of(b * 8, 8), 8)],
                send_sem=ga_send.at[which, d],
                recv_sem=ga_recv.at[which],
                device_id=(peer // B, peer % B),
                device_id_type=MESH,
            ).start()
            return carry

        lax.fori_loop(1, n, one, 0)

    def gather_recv(which, whole):
        pltpu.make_async_copy(whole, whole, ga_recv.at[which]).wait()

    def gather_sent(which, packed):
        def one(d, carry):
            pltpu.make_async_copy(packed, packed, ga_send.at[which, d]).wait()
            return carry

        lax.fori_loop(1, n, one, 0)

    beta_halo = halo_copies(0, be_ref, B0, X0, H0, Y0, 4, 3, 4, True)
    source_halo = halo_copies(1, rs_ref, S0, X0, H0, Y0, 3, 2, 4, True)
    start_all(beta_halo)
    start_all(source_halo)
    load_b.wait()

    def halve(pair, apart, slot):
        rows = pair.shape[0]
        T[slot, pl.ds(0, rows)] = pair_lanes(pair, apart)
        return 0.125 * (T[slot, pl.ds(0, rows // 2, stride=2)] + T[slot, pl.ds(1, rows // 2, stride=2)])

    def pack(planes):
        lane = lane_of(planes[0].shape) & 3
        packed = planes[3]
        for k in (2, 1, 0):
            packed = jnp.where(lane == k, planes[k], packed)
        return packed

    for p in range(X0 // 2):
        B1[H1 + p, pl.ds(HY, Y0 // 2)] = halve(
            B0[H0 + 2 * p, pl.ds(HY, Y0)] + B0[H0 + 2 * p + 1, pl.ds(HY, Y0)], 1, p
        )
    beta1_halo = halo_copies(2, B1, B1, X0 // 2, H1, Y0 // 2, 5, 5, 8, False)
    PB[...] = pack([
        halve(B1[H1 + 2 * p, pl.ds(HY, Y0 // 2)] + B1[H1 + 2 * p + 1, pl.ds(HY, Y0 // 2)], 2, p)
        for p in range(X0 // 4)
    ])

    def setup(level, Bl, CX, CY, CM, CP, Q, D, first, last, row, rows, hx, nx, ny):
        apart = 1 << level
        h = 0.5 * 0.25**level

        def plane(i, carry):
            at = pl.ds(row, rows)
            c = Bl[i, at]
            xm = Bl[i - 1, at]
            xp = Bl[i + 1, at]
            ym = Bl[i, pl.ds(row - 1, rows)]
            yp = Bl[i, pl.ds(row + 1, rows)]
            lane = lane_of(c.shape)
            low = lane >= apart
            high = lane < LANES - apart
            zm = jnp.where(low, roll(c, apart, 1), 0.0)
            zp = jnp.where(high, roll(c, -apart, 1), 0.0)
            CX[i, at] = h * (c + xm)
            CY[i, at] = h * (c + ym)
            CM[i, at] = jnp.where(low, h * (c + zm), 0.0)
            CP[i, at] = jnp.where(high, h * (c + zp), 0.0)
            d = h * (6.0 * c + ((xm + xp) + (ym + yp) + (zm + zp)))
            D[i, at] = d
            x = g * nx + i - hx
            y = lax.broadcasted_iota(jnp.int32, c.shape, 0) + (b * ny + row - HY)
            inside = (y >= 0) & (y < B * ny) & (x >= 0) & (x < G * nx)
            Q[i, at] = jnp.where(inside, W / d, 0.0)
            return carry

        lax.fori_loop(first, last, plane, 0, unroll=True)

    def across(level, V, CX, CY, CM, CP, i, row, rows):
        apart = 1 << level
        at = pl.ds(row, rows)
        up = pl.ds(row + 1, rows)
        v = V[i, at]
        total = CX[i, at] * V[i - 1, at] + CX[i + 1, at] * V[i + 1, at]
        total = total + (CY[i, at] * V[i, pl.ds(row - 1, rows)] + CY[i, up] * V[i, up])
        total = total + (CM[i, at] * roll(v, apart, 1) + CP[i, at] * roll(v, -apart, 1))
        return v, total

    def first_sweep(V, Q, S, first, last, row, rows):
        def plane(i, carry):
            V[i, pl.ds(row, rows)] = Q[i, pl.ds(row, rows)] * S[i, pl.ds(row, rows)]
            return carry

        lax.fori_loop(first, last, plane, 0, unroll=True)

    def sweep(level, V, U, S, Q, coeffs, first, last, row, rows, drop_x=0, drop_y=0):
        def plane(i, carry):
            v, total = across(level, V, *coeffs, i, row, rows)
            U[i - drop_x, pl.ds(row - drop_y, rows)] = (1.0 - W) * v + Q[i, pl.ds(row, rows)] * (
                S[i, pl.ds(row, rows)] + total
            )
            return carry

        lax.fori_loop(first, last, plane, 0, unroll=True)

    def residual(level, V, S, D, coeffs, i, row, rows):
        v, total = across(level, V, *coeffs, i, row, rows)
        return S[i, pl.ds(row, rows)] - (D[i, pl.ds(row, rows)] * v - total)

    coeffs0 = (CX0, CY0, CM0, CP0)
    coeffs1 = (CX1, CY1, CM1, CP1)
    row0, rows0 = 4, 40
    row1, rows1 = 4, 24

    recv_all(beta_halo)
    setup(0, B0, CX0, CY0, CM0, CP0, Q0, D0, 1, 23, row0, rows0, H0, X0, Y0)
    load_s.wait()
    recv_all(source_halo)
    start_all(beta1_halo)
    gather_start(0, PB, GB)
    first_sweep(V0, Q0, S0, 1, 23, row0, rows0)
    sweep(0, V0, U0, S0, Q0, coeffs0, 2, 22, row0, rows0)

    def down0(p, carry):
        i = H0 + 2 * p
        pair = residual(0, U0, S0, D0, coeffs0, i, HY, Y0) + residual(0, U0, S0, D0, coeffs0, i + 1, HY, Y0)
        S1[H1 + p, pl.ds(HY, Y0 // 2)] = halve(pair, 1, p)
        return carry

    lax.fori_loop(0, X0 // 2, down0, 0, unroll=True)
    source1_halo = halo_copies(3, S1, S1, X0 // 2, H1, Y0 // 2, 4, 4, 4, False)
    start_all(source1_halo)

    recv_all(beta1_halo)
    setup(1, B1, CX1, CY1, CM1, CP1, Q1, D1, 1, 17, row1, rows1, H1, X0 // 2, Y0 // 2)
    recv_all(source1_halo)
    first_sweep(V1, Q1, S1, 1, 17, row1, rows1)
    sweep(1, V1, U1, S1, Q1, coeffs1, 2, 16, row1, rows1)
    planes = []
    for p in range(X0 // 4):
        i = H1 + 2 * p
        pair = residual(1, U1, S1, D1, coeffs1, i, HY, Y0 // 2) + residual(1, U1, S1, D1, coeffs1, i + 1, HY, Y0 // 2)
        planes.append(halve(pair, 2, p))
    PS[...] = pack(planes)
    gather_start(1, PS, GS)

    def neighbours(v, level):
        st, zs = 1 << (level - 2), 1 << level
        before = [v[i - 1] for i in range(G)]
        after = [v[(i + 1) % G] for i in range(G)]
        if st == 4:
            xm, xp = before, after
        else:
            k = lane_of(v[0].shape) & 3
            xm = [jnp.where(k >= st, roll(v[i], st, 1), roll(before[i], st - 4, 1)) for i in range(G)]
            xp = [jnp.where(k < 4 - st, roll(v[i], -st, 1), roll(after[i], 4 - st, 1)) for i in range(G)]
        ym = [roll(a, 1, 0) for a in v]
        yp = [roll(a, -1, 0) for a in v]
        zm = [roll(a, zs, 1) for a in v]
        zp = [roll(a, -zs, 1) for a in v]
        return xm, xp, ym, yp, zm, zp

    def setup_whole(beta, C, level):
        st, zs = 1 << (level - 2), 1 << level
        h = 0.5 * 0.25**level
        near = neighbours(beta, level)
        shape = beta[0].shape
        lane = lane_of(shape)
        row = lax.broadcasted_iota(jnp.int32, shape, 0)
        for i in range(G):
            ok = [
                ((lane & 3) >= st) if i == 0 else None,
                ((lane & 3) < 4 - st) if i == G - 1 else None,
                row > 0,
                row < shape[0] - 1,
                lane >= zs,
                lane < LANES - zs,
            ]
            total = 6.0 * beta[i]
            for d in range(6):
                there = near[d][i] if ok[d] is None else jnp.where(ok[d], near[d][i], 0.0)
                total = total + there
                face = h * (beta[i] + there)
                C[d, i] = face if ok[d] is None else jnp.where(ok[d], face, 0.0)
            diag = h * total
            C[6, i] = diag
            C[7, i] = W / diag

    def sum_across(v, C, level):
        near = neighbours(v, level)
        out = []
        for i in range(G):
            out.append(
                (C[0, i] * near[0][i] + C[1, i] * near[1][i])
                + (C[2, i] * near[2][i] + C[3, i] * near[3][i])
                + (C[4, i] * near[4][i] + C[5, i] * near[5][i])
            )
        return out

    def sweep_whole(v, s, C, level):
        total = sum_across(v, C, level)
        return [(1.0 - W) * v[i] + C[7, i] * (s[i] + total[i]) for i in range(G)]

    def coarsen(v, level):
        st, zs = 1 << (level - 2), 1 << level
        rows = v[0].shape[0]
        out = []
        for i in range(G):
            E[i, pl.ds(0, rows)] = pair_lanes(pair_lanes(v[i], st), zs)
            out.append(0.125 * (E[i, pl.ds(0, rows // 2, stride=2)] + E[i, pl.ds(1, rows // 2, stride=2)]))
        return out

    def refine(v):
        rows = v[0].shape[0]
        out = []
        for i in range(G):
            E[i, pl.ds(0, rows, stride=2)] = v[i]
            E[i, pl.ds(1, rows, stride=2)] = v[i]
            out.append(E[i, pl.ds(0, 2 * rows)])
        return out

    gather_recv(0, GB)
    beta2 = [GB[i] for i in range(G)]
    setup_whole(beta2, C2, 2)
    beta3 = coarsen(beta2, 2)
    setup_whole(beta3, C3, 3)
    beta4 = coarsen(beta3, 3)
    setup_whole(beta4, C4, 4)

    gather_recv(1, GS)
    s2 = [GS[i] for i in range(G)]
    v = [C2[7, i] * s2[i] for i in range(G)]
    v = sweep_whole(v, s2, C2, 2)
    for i in range(G):
        V2[i + 1, pl.ds(8, ry2)] = v[i]
    total = sum_across(v, C2, 2)
    s3 = coarsen([s2[i] - (C2[6, i] * v[i] - total[i]) for i in range(G)], 2)
    v = [C3[7, i] * s3[i] for i in range(G)]
    v = sweep_whole(v, s3, C3, 3)
    for i in range(G):
        F3[0, i] = v[i]
        F3[1, i] = s3[i]
    total = sum_across(v, C3, 3)
    s4 = coarsen([s3[i] - (C3[6, i] * v[i] - total[i]) for i in range(G)], 3)

    def dot(a, c):
        acc = a[0] * c[0]
        for i in range(1, G):
            acc = acc + a[i] * c[i]
        part = acc[0:8]
        for j in range(8, ry4, 8):
            part = part + acc[j : j + 8]
        return jnp.sum(jnp.sum(part, axis=0, keepdims=True), axis=1, keepdims=True)

    def cg(step, carry):
        x, r, p, rr = carry
        near = sum_across(p, C4, 4)
        q = [C4[6, i] * p[i] - near[i] for i in range(G)]
        alpha = rr / dot(p, q)
        x = [x[i] + alpha * p[i] for i in range(G)]
        r = [r[i] - alpha * q[i] for i in range(G)]
        new = dot(r, r)
        ratio = new / rr
        p = [r[i] + ratio * p[i] for i in range(G)]
        return x, r, p, new

    zero = [jnp.zeros((ry4, LANES), F32) for i in range(G)]
    x4 = lax.fori_loop(0, COARSE, cg, (zero, s4, s4, dot(s4, s4)))[0]

    up = refine(x4)
    s3 = [F3[1, i] for i in range(G)]
    v = [F3[0, i] + up[i] for i in range(G)]
    for _ in range(SWEEPS):
        v = sweep_whole(v, s3, C3, 3)
    up = refine(v)
    s2 = [GS[i] for i in range(G)]
    v = [V2[i + 1, pl.ds(8, ry2)] + up[i] for i in range(G)]
    for _ in range(SWEEPS):
        v = sweep_whole(v, s2, C2, 2)
    for i in range(G):
        V2[i + 1, pl.ds(8, ry2)] = v[i]

    for x2 in range(-2, 6):
        k = x2 % 4
        window = V2[g + 1 + x2 // 4, pl.ds(pl.multiple_of(b * 8, 8), 24)]
        one = jnp.where((lane_of(window.shape) & 3) == k, window, 0.0)
        one = one + roll(one, 1 if k in (0, 2) else -1, 1)
        one = one + roll(one, 2 if k in (0, 1) else -2, 1)
        T[x2 + 2, pl.ds(0, 24)] = one
    for x2 in range(-2, 6):
        add = T[x2 + 2, pl.ds(6, 12)]
        for i in (2 * x2 + 5, 2 * x2 + 6):
            if 2 <= i < 16:
                for odd in (0, 1):
                    at = pl.ds(row1 + odd, 12, stride=2)
                    U1[i, at] = U1[i, at] + add
    sweep(1, U1, V1, S1, Q1, coeffs1, 3, 15, row1, rows1)
    sweep(1, V1, U1, S1, Q1, coeffs1, 4, 14, row1, rows1)

    def prolong0(i, carry):
        add = U1[i + 3, pl.ds(6, 20)]
        for half in (0, 1):
            for odd in (0, 1):
                at = pl.ds(row0 + odd, 20, stride=2)
                U0[2 * i + half, at] = U0[2 * i + half, at] + add
        return carry

    lax.fori_loop(1, 11, prolong0, 0, unroll=True)
    sweep(0, U0, V0, S0, Q0, coeffs0, 3, 21, row0, rows0)
    sweep(0, V0, out_ref, S0, Q0, coeffs0, 4, 20, HY, Y0, H0, HY)

    sent_all(beta_halo)
    sent_all(source_halo)
    sent_all(beta1_halo)
    sent_all(source1_halo)
    gather_sent(0, PB)
    gather_sent(1, PS)


def in_one_kernel(G, B, right_side, beta):
    level0 = pltpu.VMEM((X0 + 2 * H0, Y0 + 2 * HY, LANES), F32)
    level1 = pltpu.VMEM((X0 // 2 + 2 * H1, Y0 // 2 + 2 * HY, LANES), F32)
    return pl.pallas_call(
        functools.partial(kernel, G, B),
        out_shape=jax.ShapeDtypeStruct(right_side.shape, F32),
        in_specs=[pl.BlockSpec(memory_space=pl.ANY)] * 2,
        out_specs=pl.BlockSpec(memory_space=pltpu.VMEM),
        scratch_shapes=[level0] * 10
        + [level1] * 10
        + [
            pltpu.VMEM((8, Y0, LANES), F32),
            pltpu.VMEM((8, LANES), F32),
            pltpu.VMEM((8, LANES), F32),
            pltpu.VMEM((G, 8 * B, LANES), F32),
            pltpu.VMEM((G, 8 * B, LANES), F32),
            pltpu.VMEM((G + 2, 8 * B + 16, LANES), F32),
            pltpu.VMEM((8, G, 8 * B, LANES), F32),
            pltpu.VMEM((8, G, 4 * B, LANES), F32),
            pltpu.VMEM((8, G, 2 * B, LANES), F32),
            pltpu.VMEM((G, 8 * B, LANES), F32),
            pltpu.VMEM((2, G, 4 * B, LANES), F32),
            pltpu.SemaphoreType.DMA((4, 8)),
            pltpu.SemaphoreType.DMA((4, 8)),
            pltpu.SemaphoreType.DMA((2, G * B)),
            pltpu.SemaphoreType.DMA((2,)),
            pltpu.SemaphoreType.DMA((1,)),
            pltpu.SemaphoreType.DMA((2,)),
        ],
        compiler_params=pltpu.CompilerParams(
            collective_id=0, has_side_effects=True, vmem_limit_bytes=40 * 1024 * 1024
        ),
    )(right_side, beta)


relax_weight = 2.0 / 3.0


def with_halo(shard, sides, width):
    for axis, dim in sides:
        size, length = (lax.axis_size(axis), shard.shape[dim])
        up = [(i, (i + 1) % size) for i in range(size - 1)]
        down = [(j, i) for i, j in up]
        last = lax.slice_in_dim(shard, length - width, length, axis=dim)
        leading = lax.slice_in_dim(shard, 0, width, axis=dim)
        before = lax.ppermute(last, axis, up)
        after = lax.ppermute(leading, axis, down)
        shard = jnp.concatenate([before, shard, after], axis=dim)
    return shard


def from_partner(block, axis, apart):
    count = lax.axis_size(axis)
    route = []
    for low in range(count):
        high = low | 1 << apart
        if high != low and high < count:
            route += [(low, high), (high, low)]
    return lax.ppermute(block, axis, route)


def pad_zeros(field):
    return jnp.pad(field, 1)


def pad_local(field):
    extended = with_halo(field, (("grp", 0), ("box", 1)), 1)
    return jnp.pad(extended, ((0, 0), (0, 0), (1, 1)))


def face_coeffs(padded_beta):
    face_x = 0.5 * (padded_beta[1:, 1:-1, 1:-1] + padded_beta[:-1, 1:-1, 1:-1])
    face_y = 0.5 * (padded_beta[1:-1, 1:, 1:-1] + padded_beta[1:-1, :-1, 1:-1])
    face_z = 0.5 * (padded_beta[1:-1, 1:-1, 1:] + padded_beta[1:-1, 1:-1, :-1])
    return (face_x, face_y, face_z)


def inverse_diagonal(coeffs, scale):
    face_x, face_y, face_z = coeffs
    total = (
        face_x[:-1]
        + face_x[1:]
        + face_y[:, :-1]
        + face_y[:, 1:]
        + face_z[:, :, :-1]
        + face_z[:, :, 1:]
    )
    return 1.0 / (scale * total)


def apply_operator(padded, coeffs, scale):
    face_x, face_y, face_z = coeffs
    centre = padded[1:-1, 1:-1, 1:-1]
    total = face_x[:-1] * (centre - padded[:-2, 1:-1, 1:-1]) + face_x[1:] * (
        centre - padded[2:, 1:-1, 1:-1]
    )
    total = (
        total
        + face_y[:, :-1] * (centre - padded[1:-1, :-2, 1:-1])
        + face_y[:, 1:] * (centre - padded[1:-1, 2:, 1:-1])
    )
    total = (
        total
        + face_z[:, :, :-1] * (centre - padded[1:-1, 1:-1, :-2])
        + face_z[:, :, 1:] * (centre - padded[1:-1, 1:-1, 2:])
    )
    return scale * total


def jacobi_sweeps(field, source, coeffs, inverse, scale, count, padder):
    for sweep_index in range(count):
        field = (
            field + relax_weight * (source - apply_operator(padder(field), coeffs, scale)) * inverse
        )
    return field


def conjugate_solve(source, coeffs, scale, count):
    field = jnp.zeros_like(source)
    remain = source
    direction = source
    norm_now = jnp.sum(remain * remain)
    for step_index in range(count):
        image = apply_operator(pad_zeros(direction), coeffs, scale)
        alpha = norm_now / jnp.sum(direction * image)
        field = field + alpha * direction
        remain = remain - alpha * image
        norm_next = jnp.sum(remain * remain)
        direction = remain + norm_next / norm_now * direction
        norm_now = norm_next
    return field


def restrict_mean(field):
    size_a, size_b, size_c = field.shape
    blocks = field.reshape(size_a // 2, 2, size_b // 2, 2, size_c // 2, 2)
    return jnp.mean(blocks, axis=(1, 3, 5))


def prolong_copy(field):
    return jnp.repeat(jnp.repeat(jnp.repeat(field, 2, axis=0), 2, axis=1), 2, axis=2)


def merge_groups(pieces):
    group_index = lax.axis_index("grp")
    for bit_index in range(lax.axis_size("grp").bit_length() - 1):
        partner = from_partner(pieces, "grp", bit_index)
        upper = group_index >> bit_index & 1 == 1
        pieces = tuple(
            (
                jnp.where(
                    upper,
                    jnp.concatenate([theirs, own_piece], 0),
                    jnp.concatenate([own_piece, theirs], 0),
                )
                for own_piece, theirs in zip(pieces, partner)
            )
        )
    return pieces


def merge_boxes(pieces):
    return lax.all_gather(pieces, "box", axis=1, tiled=True)


def shards(right_side, beta):
    source = right_side
    level_beta = beta
    saved = []
    for level in range(LEVELS):
        scale = 0.25**level
        coeffs = face_coeffs(pad_local(level_beta))
        inverse = inverse_diagonal(coeffs, scale)
        field = relax_weight * source * inverse
        field = jacobi_sweeps(field, source, coeffs, inverse, scale, SWEEPS - 1, pad_local)
        residual = source - apply_operator(pad_local(field), coeffs, scale)
        saved.append((field, source, coeffs, inverse, scale))
        source = restrict_mean(residual)
        level_beta = restrict_mean(level_beta)
    low_scale = 0.25**LEVELS
    whole_source, whole_beta = merge_boxes(merge_groups((source, level_beta)))
    low_coeffs = face_coeffs(pad_zeros(whole_beta))
    whole_field = conjugate_solve(whole_source, low_coeffs, low_scale, COARSE)
    block_a, block_b, block_c = source.shape
    field = lax.dynamic_slice(
        whole_field,
        (lax.axis_index("grp") * block_a, lax.axis_index("box") * block_b, 0),
        (block_a, block_b, block_c),
    )
    for level in range(LEVELS - 1, -1, -1):
        kept, level_source, coeffs, inverse, scale = saved[level]
        field = kept + prolong_copy(field)
        field = jacobi_sweeps(field, level_source, coeffs, inverse, scale, SWEEPS, pad_local)
    return field


def solution(mesh):
    placed = P("grp", "box", None)
    G, B = mesh.shape["grp"], mesh.shape["box"]
    small = G * B <= 64 and (2 * B) % 8 == 0 and G > 1

    def local(right_side, beta):
        if small and right_side.shape == (X0, Y0, LANES):
            return in_one_kernel(G, B, right_side, beta)
        return shards(right_side, beta)

    return jax.shard_map(local, mesh=mesh, in_specs=(placed, placed), out_specs=placed, check_vma=False)
```

```python
import functools

import jax
import jax.numpy as jnp
from jax import lax
from jax.experimental import pallas as pl
from jax.experimental.pallas import tpu as pltpu
from jax.sharding import PartitionSpec as P

LEVELS = 4
SWEEPS = 2
COARSE = 8
W = 2.0 / 3.0
MESH = pl.DeviceIdType.MESH
F32 = jnp.float32

X0, Y0, LANES = 16, 32, 128
H0 = 4
H1 = 5
HY = 8
DIRS = [(dx, dy) for dx in (-1, 0, 1) for dy in (-1, 0, 1) if (dx, dy) != (0, 0)]


def roll(v, shift, axis):
    return pltpu.roll(v, shift % v.shape[axis], axis)


def lane_of(shape):
    return lax.broadcasted_iota(jnp.int32, shape, len(shape) - 1)


def pair_lanes(v, apart):
    lane = lane_of(v.shape)
    return v + jnp.where((lane & apart) == 0, roll(v, -apart, 1), roll(v, apart, 1))


def span(size, halo, step, own):
    if step == 0:
        return (halo, size), (halo, size)
    if step < 0:
        return (halo, own), (halo + size, own)
    return (halo + size - own, own), (halo - own, own)


def kernel(
    G, B, rs_ref, be_ref, out_ref,
    B0, S0, V0, U0, CX0, CY0, CM0, CP0, Q0, D0,
    B1, S1, V1, U1, CX1, CY1, CM1, CP1, Q1, D1,
    T, PB, PS, GB, GS, V2, C2, C3, C4, E, F3,
    halo_send, halo_recv, ga_send, ga_recv, rounds, loc_sem,
):
    n = G * B
    g = lax.axis_index("grp")
    b = lax.axis_index("box")
    me = g * B + b
    ry2, ry3, ry4 = 8 * B, 4 * B, 2 * B

    own0 = (pl.ds(H0, X0), pl.ds(HY, Y0))
    load_b = pltpu.make_async_copy(be_ref, B0.at[own0[0], own0[1]], loc_sem.at[0])
    load_s = pltpu.make_async_copy(rs_ref, S0.at[own0[0], own0[1]], loc_sem.at[1])
    load_b.start()
    load_s.start()

    barrier = pltpu.get_barrier_semaphore()

    partners = []
    step = 1
    while step < G:
        partners.append((step, (g + step * (1 - 2 * ((g // step) % 2)), b)))
        step *= 2
    step = 1
    while step < B:
        partners.append((step, (g, b + step * (1 - 2 * ((b // step) % 2)))))
        step *= 2
    expected = 0
    for dx, dy in DIRS:
        there = (g + dx >= 0) & (g + dx < G) & (b + dy >= 0) & (b + dy < B)
        expected = expected + there.astype(jnp.int32)

        @pl.when(there)
        def _():
            pl.semaphore_signal(barrier, inc=1, device_id=(g + dx, b + dy), device_id_type=MESH)

    for step, partner in partners:
        if step > 1:
            expected = expected + 1
            pl.semaphore_signal(barrier, inc=1, device_id=partner, device_id_type=MESH)

    def tell(k):
        pl.semaphore_signal(rounds.at[k], inc=1, device_id=partners[k][1], device_id_type=MESH)

    def hear(k):
        pl.semaphore_wait(rounds.at[k], 1)

    for ref, nx, hx, ny in ((B0, X0, H0, Y0), (S0, X0, H0, Y0), (B1, X0 // 2, H1, Y0 // 2), (S1, X0 // 2, H1, Y0 // 2)):
        rows = ny + 2 * HY
        planes = nx + 2 * hx

        @pl.when(g == 0)
        def _():
            ref[pl.ds(0, hx)] = jnp.zeros((hx, rows, LANES), F32)

        @pl.when(g == G - 1)
        def _():
            ref[pl.ds(hx + nx, hx)] = jnp.zeros((hx, rows, LANES), F32)

        @pl.when(b == 0)
        def _():
            ref[:, pl.ds(0, HY)] = jnp.zeros((planes, HY, LANES), F32)

        @pl.when(b == B - 1)
        def _():
            ref[:, pl.ds(HY + ny, HY)] = jnp.zeros((planes, HY, LANES), F32)

    V2[0] = jnp.zeros((ry2 + 16, LANES), F32)
    V2[G + 1] = jnp.zeros((ry2 + 16, LANES), F32)
    V2[:, pl.ds(0, 8)] = jnp.zeros((G + 2, 8, LANES), F32)
    V2[:, pl.ds(8 + ry2, 8)] = jnp.zeros((G + 2, 8, LANES), F32)

    pl.semaphore_wait(barrier, expected)

    def halo_copies(kind, src, dst, nx, hx, ny, deep, corner, tall, src_is_input):
        made = []
        for at, (dx, dy) in enumerate(DIRS):
            (sx, lx), (tx, _) = span(nx, hx, dx, deep if dy == 0 else corner)
            (sy, ly), (ty, _) = span(ny, HY, dy, tall)
            if src_is_input:
                sx, sy = sx - hx, sy - HY
            copy = pltpu.make_async_remote_copy(
                src_ref=src.at[pl.ds(sx, lx), pl.ds(sy, ly)],
                dst_ref=dst.at[pl.ds(tx, lx), pl.ds(ty, ly)],
                send_sem=halo_send.at[kind, at],
                recv_sem=halo_recv.at[kind, at],
                device_id=(g + dx, b + dy),
                device_id_type=MESH,
            )
            there = (g + dx >= 0) & (g + dx < G) & (b + dy >= 0) & (b + dy < B)
            here = (g - dx >= 0) & (g - dx < G) & (b - dy >= 0) & (b - dy < B)
            made.append((copy, there, here))
        return made

    def start_all(copies):
        for copy, there, _ in copies:
            pl.when(there)(copy.start)

    def recv_all(copies):
        for copy, _, here in copies:
            pl.when(here)(copy.wait_recv)

    def sent_all(copies):
        for copy, there, _ in copies:
            pl.when(there)(copy.wait_send)

    def gather_start(which, packed, whole):
        pltpu.make_async_copy(packed, whole.at[g, pl.ds(pl.multiple_of(b * 8, 8), 8)], ga_recv.at[which]).start()

        def one(d, carry):
            peer = (me + d) % n
            pltpu.make_async_remote_copy(
                src_ref=packed,
                dst_ref=whole.at[g, pl.ds(pl.multiple_of(b * 8, 8), 8)],
                send_sem=ga_send.at[which, d],
                recv_sem=ga_recv.at[which],
                device_id=(peer // B, peer % B),
                device_id_type=MESH,
            ).start()
            return carry

        lax.fori_loop(1, n, one, 0, unroll=True)

    def gather_recv(which, whole):
        pltpu.make_async_copy(whole, whole, ga_recv.at[which]).wait()

    def gather_sent(which, packed):
        def one(d, carry):
            pltpu.make_async_copy(packed, packed, ga_send.at[which, d]).wait()
            return carry

        lax.fori_loop(1, n, one, 0, unroll=True)

    beta_halo = halo_copies(0, be_ref, B0, X0, H0, Y0, 4, 3, 4, True)
    source_halo = halo_copies(1, rs_ref, S0, X0, H0, Y0, 3, 2, 4, True)
    start_all(beta_halo)
    start_all(source_halo)
    tell(0)
    load_b.wait()

    def halve(pair, apart, slot):
        rows = pair.shape[0]
        T[slot, pl.ds(0, rows)] = pair_lanes(pair, apart)
        return 0.125 * (T[slot, pl.ds(0, rows // 2, stride=2)] + T[slot, pl.ds(1, rows // 2, stride=2)])

    def pack(planes):
        lane = lane_of(planes[0].shape) & 3
        packed = planes[3]
        for k in (2, 1, 0):
            packed = jnp.where(lane == k, planes[k], packed)
        return packed

    for p in range(X0 // 2):
        B1[H1 + p, pl.ds(HY, Y0 // 2)] = halve(
            B0[H0 + 2 * p, pl.ds(HY, Y0)] + B0[H0 + 2 * p + 1, pl.ds(HY, Y0)], 1, p
        )
    beta1_halo = halo_copies(2, B1, B1, X0 // 2, H1, Y0 // 2, 5, 5, 8, False)
    PB[...] = pack([
        halve(B1[H1 + 2 * p, pl.ds(HY, Y0 // 2)] + B1[H1 + 2 * p + 1, pl.ds(HY, Y0 // 2)], 2, p)
        for p in range(X0 // 4)
    ])

    def setup(level, Bl, CX, CY, CM, CP, Q, D, first, last, row, rows, hx, nx, ny):
        apart = 1 << level
        h = 0.5 * 0.25**level

        def plane(i, carry):
            at = pl.ds(row, rows)
            c = Bl[i, at]
            xm = Bl[i - 1, at]
            xp = Bl[i + 1, at]
            ym = Bl[i, pl.ds(row - 1, rows)]
            yp = Bl[i, pl.ds(row + 1, rows)]
            lane = lane_of(c.shape)
            low = lane >= apart
            high = lane < LANES - apart
            zm = jnp.where(low, roll(c, apart, 1), 0.0)
            zp = jnp.where(high, roll(c, -apart, 1), 0.0)
            CX[i, at] = h * (c + xm)
            CY[i, at] = h * (c + ym)
            CM[i, at] = jnp.where(low, h * (c + zm), 0.0)
            CP[i, at] = jnp.where(high, h * (c + zp), 0.0)
            d = h * (6.0 * c + ((xm + xp) + (ym + yp) + (zm + zp)))
            D[i, at] = d
            x = g * nx + i - hx
            y = lax.broadcasted_iota(jnp.int32, c.shape, 0) + (b * ny + row - HY)
            inside = (y >= 0) & (y < B * ny) & (x >= 0) & (x < G * nx)
            Q[i, at] = jnp.where(inside, W / d, 0.0)
            return carry

        lax.fori_loop(first, last, plane, 0, unroll=True)

    def across(level, V, CX, CY, CM, CP, i, row, rows):
        apart = 1 << level
        at = pl.ds(row, rows)
        up = pl.ds(row + 1, rows)
        v = V[i, at]
        total = CX[i, at] * V[i - 1, at] + CX[i + 1, at] * V[i + 1, at]
        total = total + (CY[i, at] * V[i, pl.ds(row - 1, rows)] + CY[i, up] * V[i, up])
        total = total + (CM[i, at] * roll(v, apart, 1) + CP[i, at] * roll(v, -apart, 1))
        return v, total

    def first_sweep(V, Q, S, first, last, row, rows):
        def plane(i, carry):
            V[i, pl.ds(row, rows)] = Q[i, pl.ds(row, rows)] * S[i, pl.ds(row, rows)]
            return carry

        lax.fori_loop(first, last, plane, 0, unroll=True)

    def sweep(level, V, U, S, Q, coeffs, first, last, row, rows, drop_x=0, drop_y=0):
        def plane(i, carry):
            v, total = across(level, V, *coeffs, i, row, rows)
            U[i - drop_x, pl.ds(row - drop_y, rows)] = (1.0 - W) * v + Q[i, pl.ds(row, rows)] * (
                S[i, pl.ds(row, rows)] + total
            )
            return carry

        lax.fori_loop(first, last, plane, 0, unroll=True)

    def residual(level, V, S, D, coeffs, i, row, rows):
        v, total = across(level, V, *coeffs, i, row, rows)
        return S[i, pl.ds(row, rows)] - (D[i, pl.ds(row, rows)] * v - total)

    coeffs0 = (CX0, CY0, CM0, CP0)
    coeffs1 = (CX1, CY1, CM1, CP1)
    row0, rows0 = 4, 40
    row1, rows1 = 4, 24

    hear(0)
    tell(1)
    recv_all(beta_halo)
    hear(1)
    tell(2)
    setup(0, B0, CX0, CY0, CM0, CP0, Q0, D0, 1, 23, row0, rows0, H0, X0, Y0)
    load_s.wait()
    recv_all(source_halo)
    start_all(beta1_halo)
    hear(2)
    tell(3)
    first_sweep(V0, Q0, S0, 1, 23, row0, rows0)
    sweep(0, V0, U0, S0, Q0, coeffs0, 2, 22, row0, rows0)

    hear(3)
    tell(4)
    for k in range(5, len(partners)):
        hear(k - 1)
        tell(k)

    def down0(p, carry):
        i = H0 + 2 * p
        pair = residual(0, U0, S0, D0, coeffs0, i, HY, Y0) + residual(0, U0, S0, D0, coeffs0, i + 1, HY, Y0)
        S1[H1 + p, pl.ds(HY, Y0 // 2)] = halve(pair, 1, p)
        return carry

    lax.fori_loop(0, X0 // 2, down0, 0, unroll=True)
    source1_halo = halo_copies(3, S1, S1, X0 // 2, H1, Y0 // 2, 4, 4, 4, False)
    start_all(source1_halo)
    hear(len(partners) - 1)
    gather_start(0, PB, GB)

    recv_all(beta1_halo)
    setup(1, B1, CX1, CY1, CM1, CP1, Q1, D1, 1, 17, row1, rows1, H1, X0 // 2, Y0 // 2)
    recv_all(source1_halo)
    first_sweep(V1, Q1, S1, 1, 17, row1, rows1)
    sweep(1, V1, U1, S1, Q1, coeffs1, 2, 16, row1, rows1)
    planes = []
    for p in range(X0 // 4):
        i = H1 + 2 * p
        pair = residual(1, U1, S1, D1, coeffs1, i, HY, Y0 // 2) + residual(1, U1, S1, D1, coeffs1, i + 1, HY, Y0 // 2)
        planes.append(halve(pair, 2, p))
    PS[...] = pack(planes)
    gather_start(1, PS, GS)

    def neighbours(v, level):
        st, zs = 1 << (level - 2), 1 << level
        before = [v[i - 1] for i in range(G)]
        after = [v[(i + 1) % G] for i in range(G)]
        if st == 4:
            xm, xp = before, after
        else:
            k = lane_of(v[0].shape) & 3
            xm = [jnp.where(k >= st, roll(v[i], st, 1), roll(before[i], st - 4, 1)) for i in range(G)]
            xp = [jnp.where(k < 4 - st, roll(v[i], -st, 1), roll(after[i], 4 - st, 1)) for i in range(G)]
        ym = [roll(a, 1, 0) for a in v]
        yp = [roll(a, -1, 0) for a in v]
        zm = [roll(a, zs, 1) for a in v]
        zp = [roll(a, -zs, 1) for a in v]
        return xm, xp, ym, yp, zm, zp

    def setup_whole(beta, C, level):
        st, zs = 1 << (level - 2), 1 << level
        h = 0.5 * 0.25**level
        near = neighbours(beta, level)
        shape = beta[0].shape
        lane = lane_of(shape)
        row = lax.broadcasted_iota(jnp.int32, shape, 0)
        for i in range(G):
            ok = [
                ((lane & 3) >= st) if i == 0 else None,
                ((lane & 3) < 4 - st) if i == G - 1 else None,
                row > 0,
                row < shape[0] - 1,
                lane >= zs,
                lane < LANES - zs,
            ]
            total = 6.0 * beta[i]
            for d in range(6):
                there = near[d][i] if ok[d] is None else jnp.where(ok[d], near[d][i], 0.0)
                total = total + there
                face = h * (beta[i] + there)
                C[d, i] = face if ok[d] is None else jnp.where(ok[d], face, 0.0)
            diag = h * total
            C[6, i] = diag
            C[7, i] = W / diag

    def sum_across(v, C, level):
        near = neighbours(v, level)
        out = []
        for i in range(G):
            out.append(
                (C[0, i] * near[0][i] + C[1, i] * near[1][i])
                + (C[2, i] * near[2][i] + C[3, i] * near[3][i])
                + (C[4, i] * near[4][i] + C[5, i] * near[5][i])
            )
        return out

    def sweep_whole(v, s, C, level):
        total = sum_across(v, C, level)
        return [(1.0 - W) * v[i] + C[7, i] * (s[i] + total[i]) for i in range(G)]

    def coarsen(v, level):
        st, zs = 1 << (level - 2), 1 << level
        rows = v[0].shape[0]
        out = []
        for i in range(G):
            E[i, pl.ds(0, rows)] = pair_lanes(pair_lanes(v[i], st), zs)
            out.append(0.125 * (E[i, pl.ds(0, rows // 2, stride=2)] + E[i, pl.ds(1, rows // 2, stride=2)]))
        return out

    def refine(v):
        rows = v[0].shape[0]
        out = []
        for i in range(G):
            E[i, pl.ds(0, rows, stride=2)] = v[i]
            E[i, pl.ds(1, rows, stride=2)] = v[i]
            out.append(E[i, pl.ds(0, 2 * rows)])
        return out

    gather_recv(0, GB)
    beta2 = [GB[i] for i in range(G)]
    setup_whole(beta2, C2, 2)
    beta3 = coarsen(beta2, 2)
    setup_whole(beta3, C3, 3)
    beta4 = coarsen(beta3, 3)
    setup_whole(beta4, C4, 4)

    gather_recv(1, GS)
    s2 = [GS[i] for i in range(G)]
    v = [C2[7, i] * s2[i] for i in range(G)]
    v = sweep_whole(v, s2, C2, 2)
    for i in range(G):
        V2[i + 1, pl.ds(8, ry2)] = v[i]
    total = sum_across(v, C2, 2)
    s3 = coarsen([s2[i] - (C2[6, i] * v[i] - total[i]) for i in range(G)], 2)
    v = [C3[7, i] * s3[i] for i in range(G)]
    v = sweep_whole(v, s3, C3, 3)
    for i in range(G):
        F3[0, i] = v[i]
        F3[1, i] = s3[i]
    total = sum_across(v, C3, 3)
    s4 = coarsen([s3[i] - (C3[6, i] * v[i] - total[i]) for i in range(G)], 3)

    def dot(a, c):
        acc = a[0] * c[0]
        for i in range(1, G):
            acc = acc + a[i] * c[i]
        part = acc[0:8]
        for j in range(8, ry4, 8):
            part = part + acc[j : j + 8]
        return jnp.sum(jnp.sum(part, axis=0, keepdims=True), axis=1, keepdims=True)

    def cg(step, carry):
        x, r, p, rr = carry
        near = sum_across(p, C4, 4)
        q = [C4[6, i] * p[i] - near[i] for i in range(G)]
        alpha = rr / dot(p, q)
        x = [x[i] + alpha * p[i] for i in range(G)]
        r = [r[i] - alpha * q[i] for i in range(G)]
        new = dot(r, r)
        ratio = new / rr
        p = [r[i] + ratio * p[i] for i in range(G)]
        return x, r, p, new

    zero = [jnp.zeros((ry4, LANES), F32) for i in range(G)]
    x4 = lax.fori_loop(0, COARSE, cg, (zero, s4, s4, dot(s4, s4)), unroll=True)[0]

    up = refine(x4)
    s3 = [F3[1, i] for i in range(G)]
    v = [F3[0, i] + up[i] for i in range(G)]
    for _ in range(SWEEPS):
        v = sweep_whole(v, s3, C3, 3)
    up = refine(v)
    s2 = [GS[i] for i in range(G)]
    v = [V2[i + 1, pl.ds(8, ry2)] + up[i] for i in range(G)]
    for _ in range(SWEEPS):
        v = sweep_whole(v, s2, C2, 2)
    for i in range(G):
        V2[i + 1, pl.ds(8, ry2)] = v[i]

    for x2 in range(-2, 6):
        k = x2 % 4
        window = V2[g + 1 + x2 // 4, pl.ds(pl.multiple_of(b * 8, 8), 24)]
        one = jnp.where((lane_of(window.shape) & 3) == k, window, 0.0)
        one = one + roll(one, 1 if k in (0, 2) else -1, 1)
        one = one + roll(one, 2 if k in (0, 1) else -2, 1)
        T[x2 + 2, pl.ds(0, 24)] = one
    for x2 in range(-2, 6):
        add = T[x2 + 2, pl.ds(6, 12)]
        for i in (2 * x2 + 5, 2 * x2 + 6):
            if 2 <= i < 16:
                for odd in (0, 1):
                    at = pl.ds(row1 + odd, 12, stride=2)
                    U1[i, at] = U1[i, at] + add
    sweep(1, U1, V1, S1, Q1, coeffs1, 3, 15, row1, rows1)
    sweep(1, V1, U1, S1, Q1, coeffs1, 4, 14, row1, rows1)

    def prolong0(i, carry):
        add = U1[i + 3, pl.ds(6, 20)]
        for half in (0, 1):
            for odd in (0, 1):
                at = pl.ds(row0 + odd, 20, stride=2)
                U0[2 * i + half, at] = U0[2 * i + half, at] + add
        return carry

    lax.fori_loop(1, 11, prolong0, 0, unroll=True)
    sweep(0, U0, V0, S0, Q0, coeffs0, 3, 21, row0, rows0)
    sweep(0, V0, out_ref, S0, Q0, coeffs0, 4, 20, HY, Y0, H0, HY)

    sent_all(beta_halo)
    sent_all(source_halo)
    sent_all(beta1_halo)
    sent_all(source1_halo)
    gather_sent(0, PB)
    gather_sent(1, PS)


def in_one_kernel(G, B, right_side, beta):
    level0 = pltpu.VMEM((X0 + 2 * H0, Y0 + 2 * HY, LANES), F32)
    level1 = pltpu.VMEM((X0 // 2 + 2 * H1, Y0 // 2 + 2 * HY, LANES), F32)
    return pl.pallas_call(
        functools.partial(kernel, G, B),
        out_shape=jax.ShapeDtypeStruct(right_side.shape, F32),
        in_specs=[pl.BlockSpec(memory_space=pl.ANY)] * 2,
        out_specs=pl.BlockSpec(memory_space=pltpu.VMEM),
        scratch_shapes=[level0] * 10
        + [level1] * 10
        + [
            pltpu.VMEM((8, Y0, LANES), F32),
            pltpu.VMEM((8, LANES), F32),
            pltpu.VMEM((8, LANES), F32),
            pltpu.VMEM((G, 8 * B, LANES), F32),
            pltpu.VMEM((G, 8 * B, LANES), F32),
            pltpu.VMEM((G + 2, 8 * B + 16, LANES), F32),
            pltpu.VMEM((8, G, 8 * B, LANES), F32),
            pltpu.VMEM((8, G, 4 * B, LANES), F32),
            pltpu.VMEM((8, G, 2 * B, LANES), F32),
            pltpu.VMEM((G, 8 * B, LANES), F32),
            pltpu.VMEM((2, G, 4 * B, LANES), F32),
            pltpu.SemaphoreType.DMA((4, 8)),
            pltpu.SemaphoreType.DMA((4, 8)),
            pltpu.SemaphoreType.DMA((2, G * B)),
            pltpu.SemaphoreType.DMA((2,)),
            pltpu.SemaphoreType.REGULAR((8,)),
            pltpu.SemaphoreType.DMA((2,)),
        ],
        compiler_params=pltpu.CompilerParams(
            collective_id=0, has_side_effects=True, vmem_limit_bytes=40 * 1024 * 1024
        ),
    )(right_side, beta)


relax_weight = 2.0 / 3.0


def with_halo(shard, sides, width):
    for axis, dim in sides:
        size, length = (lax.axis_size(axis), shard.shape[dim])
        up = [(i, (i + 1) % size) for i in range(size - 1)]
        down = [(j, i) for i, j in up]
        last = lax.slice_in_dim(shard, length - width, length, axis=dim)
        leading = lax.slice_in_dim(shard, 0, width, axis=dim)
        before = lax.ppermute(last, axis, up)
        after = lax.ppermute(leading, axis, down)
        shard = jnp.concatenate([before, shard, after], axis=dim)
    return shard


def from_partner(block, axis, apart):
    count = lax.axis_size(axis)
    route = []
    for low in range(count):
        high = low | 1 << apart
        if high != low and high < count:
            route += [(low, high), (high, low)]
    return lax.ppermute(block, axis, route)


def pad_zeros(field):
    return jnp.pad(field, 1)


def pad_local(field):
    extended = with_halo(field, (("grp", 0), ("box", 1)), 1)
    return jnp.pad(extended, ((0, 0), (0, 0), (1, 1)))


def face_coeffs(padded_beta):
    face_x = 0.5 * (padded_beta[1:, 1:-1, 1:-1] + padded_beta[:-1, 1:-1, 1:-1])
    face_y = 0.5 * (padded_beta[1:-1, 1:, 1:-1] + padded_beta[1:-1, :-1, 1:-1])
    face_z = 0.5 * (padded_beta[1:-1, 1:-1, 1:] + padded_beta[1:-1, 1:-1, :-1])
    return (face_x, face_y, face_z)


def inverse_diagonal(coeffs, scale):
    face_x, face_y, face_z = coeffs
    total = (
        face_x[:-1]
        + face_x[1:]
        + face_y[:, :-1]
        + face_y[:, 1:]
        + face_z[:, :, :-1]
        + face_z[:, :, 1:]
    )
    return 1.0 / (scale * total)


def apply_operator(padded, coeffs, scale):
    face_x, face_y, face_z = coeffs
    centre = padded[1:-1, 1:-1, 1:-1]
    total = face_x[:-1] * (centre - padded[:-2, 1:-1, 1:-1]) + face_x[1:] * (
        centre - padded[2:, 1:-1, 1:-1]
    )
    total = (
        total
        + face_y[:, :-1] * (centre - padded[1:-1, :-2, 1:-1])
        + face_y[:, 1:] * (centre - padded[1:-1, 2:, 1:-1])
    )
    total = (
        total
        + face_z[:, :, :-1] * (centre - padded[1:-1, 1:-1, :-2])
        + face_z[:, :, 1:] * (centre - padded[1:-1, 1:-1, 2:])
    )
    return scale * total


def jacobi_sweeps(field, source, coeffs, inverse, scale, count, padder):
    for sweep_index in range(count):
        field = (
            field + relax_weight * (source - apply_operator(padder(field), coeffs, scale)) * inverse
        )
    return field


def conjugate_solve(source, coeffs, scale, count):
    field = jnp.zeros_like(source)
    remain = source
    direction = source
    norm_now = jnp.sum(remain * remain)
    for step_index in range(count):
        image = apply_operator(pad_zeros(direction), coeffs, scale)
        alpha = norm_now / jnp.sum(direction * image)
        field = field + alpha * direction
        remain = remain - alpha * image
        norm_next = jnp.sum(remain * remain)
        direction = remain + norm_next / norm_now * direction
        norm_now = norm_next
    return field


def restrict_mean(field):
    size_a, size_b, size_c = field.shape
    blocks = field.reshape(size_a // 2, 2, size_b // 2, 2, size_c // 2, 2)
    return jnp.mean(blocks, axis=(1, 3, 5))


def prolong_copy(field):
    return jnp.repeat(jnp.repeat(jnp.repeat(field, 2, axis=0), 2, axis=1), 2, axis=2)


def merge_groups(pieces):
    group_index = lax.axis_index("grp")
    for bit_index in range(lax.axis_size("grp").bit_length() - 1):
        partner = from_partner(pieces, "grp", bit_index)
        upper = group_index >> bit_index & 1 == 1
        pieces = tuple(
            (
                jnp.where(
                    upper,
                    jnp.concatenate([theirs, own_piece], 0),
                    jnp.concatenate([own_piece, theirs], 0),
                )
                for own_piece, theirs in zip(pieces, partner)
            )
        )
    return pieces


def merge_boxes(pieces):
    return lax.all_gather(pieces, "box", axis=1, tiled=True)


def shards(right_side, beta):
    source = right_side
    level_beta = beta
    saved = []
    for level in range(LEVELS):
        scale = 0.25**level
        coeffs = face_coeffs(pad_local(level_beta))
        inverse = inverse_diagonal(coeffs, scale)
        field = relax_weight * source * inverse
        field = jacobi_sweeps(field, source, coeffs, inverse, scale, SWEEPS - 1, pad_local)
        residual = source - apply_operator(pad_local(field), coeffs, scale)
        saved.append((field, source, coeffs, inverse, scale))
        source = restrict_mean(residual)
        level_beta = restrict_mean(level_beta)
    low_scale = 0.25**LEVELS
    whole_source, whole_beta = merge_boxes(merge_groups((source, level_beta)))
    low_coeffs = face_coeffs(pad_zeros(whole_beta))
    whole_field = conjugate_solve(whole_source, low_coeffs, low_scale, COARSE)
    block_a, block_b, block_c = source.shape
    field = lax.dynamic_slice(
        whole_field,
        (lax.axis_index("grp") * block_a, lax.axis_index("box") * block_b, 0),
        (block_a, block_b, block_c),
    )
    for level in range(LEVELS - 1, -1, -1):
        kept, level_source, coeffs, inverse, scale = saved[level]
        field = kept + prolong_copy(field)
        field = jacobi_sweeps(field, level_source, coeffs, inverse, scale, SWEEPS, pad_local)
    return field


def solution(mesh):
    placed = P("grp", "box", None)
    G, B = mesh.shape["grp"], mesh.shape["box"]
    small = (G, B) in ((4, 8), (8, 8), (4, 16), (8, 4), (2, 16))

    def local(right_side, beta):
        if small and right_side.shape == (X0, Y0, LANES):
            return in_one_kernel(G, B, right_side, beta)
        return shards(right_side, beta)

    return jax.shard_map(local, mesh=mesh, in_specs=(placed, placed), out_specs=placed, check_vma=False)
```
